128 devices in a mesh: run: 8 (over y, x_lo), mz: 16 (over z, x_hi, core).
Axes of the slice: x: 4 (x_hi: 2, x_lo: 2; x = x_hi * 2 + x_lo), y: 4, z: 4, core: 2. Of those that a mesh axis runs over, the one named last changes fastest.
Arguments:
- spectra: bfloat16 [98304, 4096], P('run', 'mz'), may hold values from -6 to 6
- mz_factor: bfloat16 [4096, 128], P('mz'), may hold values from -0.1125 to 0.1125
- mixing: float32 [128, 128], replicated, may hold values from -1 to 2, as said below
- run_weights: float32 [96, 128], P('run'), may hold values from 0.5 to 6
- block_count: int32 [8, 12], P('run'), may hold values from 1 to 8, 48 in all within a row
- trim_scans: int32 [8, 12], P('run'), may hold values from 0 to 56
Outputs:
- new_mz: float32 [4096, 128], P('mz')
- new_weights: float32 [96, 128], P('run')
The draws below stay inside these ranges and needn't reach their ends.
Inputs may be any that keep to these rules, and one draw needn't show every extreme that they name: `mixing`: about the identity plus a dense part.
All inputs are finite; a program needn't handle non-finite values.
Results may differ from the reference program's by a relative error of at most 0.00071.
Values may be sent and summed in bfloat16 or wider, within the bound.
A program may use at most 128 MiB of HBM per device.

```python
import math
import jax
import jax.numpy as jnp
import numpy as np
from jax import lax

R = 128
J = 4096
BLOCK = 256
MAXB = 8
NSTEPS = 8
RUN_DEV = 12
SLOTS = 48
RUNS = 96
SCANS = 98304
N_RUN = 8


def draw_mz_factor(key, part):
    key = jax.random.fold_in(key, 11)
    rising = 0.6 + 1.2 * jnp.arange(J, dtype=jnp.float32)[:, None] / (J - 1)
    base_draw = jax.random.truncated_normal(key, -4.0, 4.0, (J, R), jnp.float32)
    return (base_draw * rising / jnp.sqrt(jnp.float32(J))).astype(jnp.bfloat16)


def draw_mixing(key, part):
    key = jax.random.fold_in(key, 23)
    second_key = jax.random.fold_in(key, 1)
    diagonal = jnp.ones((R,), jnp.float32)
    dense = jax.random.truncated_normal(second_key, -4.0, 4.0, (R, R), jnp.float32)
    return jnp.diag(diagonal) + 0.3 * dense / jnp.sqrt(jnp.float32(R))


def draw_run_weights(key, part):
    key = jax.random.fold_in(key, 37)
    rising = 1.0 + 2.0 * jnp.arange(RUNS, dtype=jnp.float32)[:, None] / max(RUNS - 1, 1)
    base_draw = jnp.exp(jax.random.uniform(key, (RUNS, R), jnp.float32, -0.6931, 0.6931))
    return jnp.clip(base_draw, 0.5, 2.0) * rising


def with_ends(values, key, low, top_value):
    spot = [jax.random.randint(jax.random.fold_in(key, axis), (), 0, length) for axis, length in enumerate(values.shape)]
    widest = values.shape.index(max(values.shape))
    beside = spot[:widest] + [(spot[widest] + 1) % values.shape[widest]] + spot[widest + 1:]
    return values.at[tuple(spot)].set(low).at[tuple(beside)].set(top_value)


def level_of(rng, extent, cuts, low, largest):
    level = 1.0
    for position, blocks in cuts:
        steps = jax.random.uniform(jax.random.fold_in(jax.random.fold_in(rng, 6), position), (blocks,), jnp.float32, low / len(cuts), largest / len(cuts))
        level = level * jnp.repeat(jnp.exp(steps), extent[position] // blocks).reshape((-1,) + (1,) * (len(extent) - 1 - position))
    return level


def split_up(amount, total, reach, slope):
    weights = [(1 << 20) // math.isqrt(grade ** slope) + 1 for grade in range(2, amount + 1)]
    rest, given = total - reach - (amount - 1), [1] * (amount - 1)
    while rest > 0:
        candidates = [i for i in range(amount - 1) if given[i] < reach]
        pool, remaining = sum([weights[i] for i in candidates]), rest
        for i in candidates:
            extra = min(reach - given[i], max(1, remaining * weights[i] // pool), rest)
            given[i] = given[i] + extra
            rest = rest - extra
    return np.array([reach] + given)


def uneven(key, count, total, limit, lean):
    if count == 2:
        one = jax.random.randint(key, (), max(1, total - limit), min(limit, total - 1) + 1)
        return jnp.stack([one, total - one])
    sizes = jnp.asarray(split_up(count, total, limit, lean), jnp.int32)
    twos = (count - 1) // 2
    source_of, taker = sizes[1:1 + 2 * twos:2], sizes[2:2 + 2 * twos:2]
    margin = jnp.minimum(source_of - 1, limit - taker)
    shifted = jax.random.randint(jax.random.fold_in(key, 1), (twos,), 0, 1 << 20) % (margin + 1)
    sizes = sizes.at[1:1 + 2 * twos:2].set(source_of - shifted).at[2:2 + 2 * twos:2].set(taker + shifted)
    return sizes[jax.random.permutation(jax.random.fold_in(key, 2), count)]


def centred(stream_key, extent, deviation, limit, cuts=(), held_as=jnp.bfloat16):
    array = jax.random.normal(stream_key, extent, jnp.float32) * deviation
    if len(cuts) > 0:
        array = level_of(stream_key, extent, cuts, -0.22, 0.18) * array
    return jnp.clip(array, min=-limit, max=limit).astype(held_as)


def setup_inputs(seed: int = 0) -> dict:
    splits = jax.random.split(jax.random.key(seed), 7)
    spectra = centred(splits[0], (SCANS, J), 1.0, 6.0, ((0, 8), (1, 16)))
    mz_factor = draw_mz_factor(jax.random.fold_in(splits[6], 71), 0)
    mixing = draw_mixing(jax.random.fold_in(splits[6], 71), 0)
    run_weights = draw_run_weights(jax.random.fold_in(splits[6], 71), 0)
    block_count = jax.vmap(lambda own: uneven(own, RUN_DEV, SLOTS, MAXB, 2))(jax.random.split(splits[4], N_RUN)).reshape((N_RUN, RUN_DEV)).astype(jnp.int32)
    trim_scans = with_ends(jax.random.randint(splits[5], (N_RUN, RUN_DEV), 0, BLOCK * 7 // 32 + 1), jax.random.fold_in(splits[5], 1), 0, (BLOCK * 7 // 32 + 1) - 1).astype(jnp.int32)
    return {"spectra": spectra, "mz_factor": mz_factor, "mixing": mixing, "run_weights": run_weights, "block_count": block_count, "trim_scans": trim_scans}


highest = lax.Precision.HIGHEST

def run_layout(counts, trims):
    starts = jnp.cumsum(counts).astype(jnp.int32) - counts
    block_ids = jnp.arange(SLOTS, dtype=jnp.int32)
    member = (block_ids[None, :] >= starts[:, None]) & (block_ids[None, :] < (starts + counts)[:, None])
    final_block = block_ids[None, :] == (starts + counts - 1)[:, None]
    scan_limit = BLOCK - lax.optimization_barrier(jnp.sum(jnp.where(final_block, trims[:, None], 0), axis=0)).astype(jnp.int32)
    return (member.astype(jnp.float32), scan_limit)

def solve_right(matrix, values):
    lower = jnp.linalg.cholesky(matrix)
    return jax.scipy.linalg.cho_solve((lower, True), values.T).T

def group_run(pieces, mz_factor, mixing):
    spectra_part, weight_part, count_part, trim_part = pieces
    member, scan_limit = run_layout(count_part, trim_part)
    live_rows = jnp.arange(BLOCK, dtype=jnp.int32)[None, :] < scan_limit[:, None]
    masked = jnp.where(live_rows.reshape(-1)[:, None], spectra_part, jnp.zeros((), spectra_part.dtype))
    scores = jnp.dot(masked.astype(jnp.float32), mz_factor.astype(jnp.float32), preferred_element_type=jnp.float32)
    block_weights = jnp.dot(member.T, weight_part, precision=highest)
    scaled = scores.reshape(SLOTS, BLOCK, R) * block_weights[:, None, :]
    target = jnp.einsum('bir,sr->bis', scaled, mixing, precision=highest)
    square_sums = jnp.dot(member, lax.optimization_barrier(jnp.sum(target * target, axis=(1, 2))), precision=highest)
    run_norm = jnp.sqrt(square_sums + 1e-06)
    iterate = target / jnp.dot(member.T, run_norm, precision=highest)[:, None, None]
    identity = jnp.eye(R, dtype=jnp.float32)
    for sweep in range(NSTEPS):
        block_grams = jnp.einsum('bir,bis->brs', iterate, iterate, precision=highest)
        run_grams = jnp.einsum('kb,brs->krs', member, block_grams, precision=highest)
        coefficient = 1.5 * identity[None] - 0.5 * run_grams
        spread = jnp.einsum('kb,krs->brs', member, coefficient, precision=highest)
        iterate = jnp.einsum('bir,brs->bis', iterate, spread, precision=highest)
    polar_rows = iterate.astype(jnp.bfloat16).astype(jnp.float32)
    blocks = masked.reshape(SLOTS, BLOCK, J).astype(jnp.float32)
    block_proj = jnp.einsum('bir,bij->brj', polar_rows, blocks, precision=highest)
    return jnp.einsum('kb,brj->krj', member, block_proj, precision=highest)

def reference(spectra, mz_factor, mixing, run_weights, block_count, trim_scans):
    pieces = (spectra.reshape(N_RUN, SLOTS * BLOCK, J), run_weights.reshape(N_RUN, RUN_DEV, R), block_count, trim_scans)
    projected = lax.map(lambda item: group_run(item, mz_factor, mixing), pieces)
    projected = projected.reshape(RUNS, R, J)
    mix_gram = jnp.dot(mixing.T, mixing, precision=highest)
    weight_gram = jnp.dot(run_weights.T, run_weights, precision=highest)
    scaled_mix = mixing[None, :, :] * run_weights[:, None, :]
    gathered = jnp.einsum('kij,kir->jr', projected, scaled_mix, precision=highest)
    new_mz = solve_right(weight_gram * mix_gram, gathered)
    mz_gram = jnp.dot(new_mz.T, new_mz, precision=highest)
    along_mz = jnp.einsum('kij,jr->kir', projected, new_mz, precision=highest)
    equation = lax.optimization_barrier(jnp.sum(along_mz * mixing[None, :, :], axis=1))
    new_weights = solve_right(mz_gram * mix_gram, equation)
    return (new_mz, new_weights)
```

```python
import functools

import jax
import jax.numpy as jnp
from jax import lax
from jax.experimental import pallas as pl
from jax.experimental.pallas import tpu as pltpu
from jax.sharding import PartitionSpec as P

R = 128
BLOCK = 256
NSTEPS = 8
RUN_DEV = 12
SLOTS = 48
MAXB = 8
CHIPS = 8
N_RUN = 8
OWN = 3
TILES = 6
ROWS = TILES * R
CODED = ROWS + 16
WIDTH = 256
LEVELS = 32000.0
INV_STEPS = 26

MESH = pl.DeviceIdType.MESH
F32 = jnp.float32
BF16 = jnp.bfloat16


def split(x):
    hi = x.astype(BF16)
    return hi, (x - hi.astype(F32)).astype(BF16)


def mm(x, y):
    xh, xl = split(x)
    yh, yl = split(y)
    right = jnp.concatenate([yh, yl], axis=1)
    out = jnp.dot(
        jnp.concatenate([xh, xl], axis=1),
        jnp.concatenate([right, right], axis=0),
        preferred_element_type=F32,
    )
    return out[:, :R] + out[:, R:]


def mm_nt(x, y):
    xh, xl = split(x)
    yh, yl = split(y)
    right = jnp.concatenate(
        [jnp.concatenate([yh, yh], axis=1), jnp.concatenate([yl, yl], axis=1)], axis=0
    )
    out = lax.dot_general(
        jnp.concatenate([xh, xl], axis=1),
        right,
        (((1,), (1,)), ((), ())),
        preferred_element_type=F32,
    )
    return out[:, :R] + out[:, R:]


def stack_left(x):
    xh, xl = split(x)
    return jnp.concatenate(
        [jnp.concatenate([xh, xh], axis=1), jnp.concatenate([xl, xl], axis=1)], axis=0
    )


def wide(left, y):
    yh, yl = split(y)
    out = jnp.dot(left, jnp.concatenate([yh, yl], axis=0), preferred_element_type=F32)
    return out[:R] + out[R:]


def self_gram(x):
    xh, xl = split(x)
    both = jnp.concatenate([xh, xl], axis=0)
    out = lax.dot_general(both, both, (((1,), (1,)), ((), ())), preferred_element_type=F32)
    return out[:R, :R] + out[:R, R:] + out[R:, :R] + out[R:, R:]


def eye_mask():
    return lax.broadcasted_iota(jnp.int32, (R, R), 0) == lax.broadcasted_iota(jnp.int32, (R, R), 1)


def inverse_start(matrix):
    eye = eye_mask()
    diagonal = jnp.where(eye, matrix, 0.0)
    row = lax.rsqrt(jnp.sum(diagonal, axis=0, keepdims=True))
    column = lax.rsqrt(jnp.sum(diagonal, axis=1, keepdims=True))
    scaled = matrix * row * column
    bound = jnp.max(jnp.sum(jnp.abs(scaled), axis=0, keepdims=True), axis=1, keepdims=True)
    alpha = 1.0 / bound
    unit = jnp.where(eye, 1.0, 0.0)
    return scaled, row, column, alpha * unit, unit - alpha * scaled


def inverse_step(x, r):
    out = mm(jnp.concatenate([x, r], axis=0), r)
    return x + out[:R], out[R:]


def inverse_polish(scaled, x):
    residual = jnp.where(eye_mask(), 1.0, 0.0) - mm(scaled, x)
    return x + mm(x, residual)


def encode(x):
    top = jnp.max(jnp.max(jnp.abs(x), axis=0), axis=0, keepdims=True)
    code = jnp.ceil(jnp.log(jnp.maximum(top, 1e-30)) * 64.0)
    factor = jnp.exp(code * (-1.0 / 64.0)) * LEVELS
    return jnp.round(x * factor[None]).astype(jnp.int32).astype(jnp.int16), code


def decode_scale(code_rows):
    return jnp.exp(code_rows.astype(F32)[:1] * (1.0 / 64.0)) * (1.0 / LEVELS)


def main_kernel(
    x_hbm, v_ref, h_ref, w_ref, count_ref, trim_ref,
    nmt_ref, sums_ref,
    xv, vt, dsend, drecv, keep, rs_send, rs_recv, acc, agbuf, st, gram, gs, qs, ft, zb, us,
    wall, cinv, wt, bpart, brecv, ball, e_part, e_sib, e_half, e_recv, e_out, e_fin,
    xsem, d_s, d_r, rs_s, rs_r, ag_s, ag_r, fw_s, fw_r, w_s, w_r, b1_s, b1_r, b2_s, b2_r,
    e1_s, e1_r, e2_s, e2_r, e3_s, e3_r,
):
    run = lax.axis_index("run")
    me = lax.axis_index("mz")
    chip = lax.div(me, 2)
    core = lax.rem(me, 2)
    sibling = (run, chip * 2 + 1 - core)

    def chip_at(step):
        return lax.rem(chip + step, CHIPS)

    def peer(step):
        return (run, chip_at(step) * 2 + core)

    def run_peer(step):
        return (lax.rem(run + step, N_RUN), me)

    def x_copy(step, side):
        chunk = chip_at(step + 1) * 2 + (core if side else 1 - core)
        rows = pl.ds(pl.multiple_of(chunk * ROWS, ROWS), ROWS)
        return pltpu.make_async_copy(x_hbm.at[rows], xv.at[rows], xsem.at[step * 2 + side])

    for step in range(CHIPS):
        x_copy(step, 0).start()
        x_copy(step, 1).start()

    barrier = pltpu.get_barrier_semaphore()
    pl.semaphore_signal(barrier, inc=1, device_id=sibling, device_id_type=MESH)
    for step in range(1, CHIPS):
        pl.semaphore_signal(barrier, inc=1, device_id=peer(step), device_id_type=MESH)
        pl.semaphore_signal(barrier, inc=1, device_id=run_peer(step), device_id_type=MESH)

    vt[...] = v_ref[...].astype(F32).T.astype(BF16)
    weights = jnp.concatenate([w_ref[...], jnp.zeros((16 - RUN_DEV, R), F32)], axis=0)
    wall[run] = weights

    pl.semaphore_wait(barrier, 2 * CHIPS - 1)

    def send(src, dst, s_sem, r_sem, device):
        return pltpu.make_async_remote_copy(
            src_ref=src, dst_ref=dst, send_sem=s_sem, recv_sem=r_sem,
            device_id=device, device_id_type=MESH,
        )

    def run_from(step):
        return lax.rem(run + N_RUN - step, N_RUN)

    def chip_from(step):
        return lax.rem(chip + CHIPS - step, CHIPS)

    def w_copy(step, slot=run):
        return send(wall.at[slot], wall.at[slot], w_s.at[step], w_r.at[step], run_peer(step))

    for step in range(1, N_RUN):
        w_copy(step).start()

    def partial(chunk, dst, step):
        for i in range(OWN):
            rows = pl.ds(pl.multiple_of(chunk * ROWS + i * BLOCK, BLOCK), BLOCK)
            out = lax.dot_general(
                vt[...], xv[rows, :], (((1,), (1,)), ((), ())), preferred_element_type=F32
            )
            dst[step, 2 * i] = out[:, :R]
            dst[step, 2 * i + 1] = out[:, R:]

    def d_copy(step):
        return send(dsend.at[step], drecv.at[step], d_s.at[step], d_r.at[step], sibling)

    def rs_copy(step):
        return send(rs_send.at[step], rs_recv.at[step], rs_s.at[step], rs_r.at[step], peer(step + 1))

    def reduce_body(step, carry):
        @pl.when(step < CHIPS)
        def _():
            target = chip_at(step + 1)
            x_copy(step, 0).wait()
            partial(target * 2 + 1 - core, dsend, step)
            d_copy(step).start()
            x_copy(step, 1).wait()
            partial(target * 2 + core, keep, step)

        @pl.when((step >= 1) & (step < CHIPS))
        def _():
            last = step - 1
            d_copy(last).wait_recv()
            values, code = encode(keep[last] + drecv[last])
            rs_send[last, :ROWS] = values.reshape(ROWS, R)
            rs_send[last, ROWS:] = jnp.broadcast_to(code, (16, R)).astype(jnp.int32).astype(jnp.int16)
            rs_copy(last).start()

        return carry

    lax.fori_loop(0, CHIPS, reduce_body, 0)

    for step in range(1, N_RUN):
        w_copy(step, run_from(step)).wait_recv()
    all_weights = wall[...].reshape(N_RUN * 16, R)
    h = h_ref[...]
    ht = h.T
    mix_gram = mm(ht, h)
    c_matrix = mm(all_weights.T, all_weights) * mix_gram
    scaled, row, column, x0, r0 = inverse_start(c_matrix)

    def inv_body(i, carry):
        return inverse_step(*carry)

    x0, r0 = lax.fori_loop(0, INV_STEPS, inv_body, (x0, r0))
    x0 = inverse_polish(scaled, x0)
    x0 = inverse_polish(scaled, x0)
    cinv[...] = x0 * row * column
    own_weights = jnp.concatenate([weights, jnp.zeros((R - 16, R), F32)], axis=0)
    wt[...] = own_weights.T

    d_copy(CHIPS - 1).wait_recv()
    acc[...] = keep[CHIPS - 1] + drecv[CHIPS - 1]

    def sum_body(step, carry):
        rs_copy(step).wait_recv()
        scale = decode_scale(rs_recv[step, ROWS:])
        acc[...] += rs_recv[step, :ROWS].astype(F32).reshape(TILES, R, R) * scale[None]
        return carry

    lax.fori_loop(0, CHIPS - 1, sum_body, 0)

    starts = []
    total = jnp.int32(0)
    for k in range(RUN_DEV):
        starts.append(total)
        total = total + count_ref[0, k]
    ends = starts[1:] + [total]
    lane = lax.broadcasted_iota(jnp.int32, (1, R), 1)
    for i in range(OWN):
        block = me * OWN + i
        limit = jnp.int32(BLOCK)
        for k in range(RUN_DEV):
            limit = limit - jnp.where(block == ends[k] - 1, trim_ref[0, k], 0)
        acc[2 * i] = jnp.where(lane < limit, acc[2 * i], 0.0)
        acc[2 * i + 1] = jnp.where(lane + R < limit, acc[2 * i + 1], 0.0)

    values, code = encode(acc[...])
    agbuf[me, :ROWS] = values.reshape(ROWS, R)
    agbuf[me, ROWS:] = jnp.broadcast_to(code, (16, R)).astype(jnp.int32).astype(jnp.int16)

    def ag_copy(step, slot=me):
        return send(agbuf.at[slot], agbuf.at[slot], ag_s.at[step], ag_r.at[step], peer(step))

    def fw_copy(step, side=core):
        slot = chip_from(step) * 2 + side
        return send(agbuf.at[slot], agbuf.at[slot], fw_s.at[step], fw_r.at[step], sibling)

    for step in range(1, CHIPS):
        ag_copy(step).start()

    def take(slot):
        scale = decode_scale(agbuf[slot, ROWS:])
        for i in range(OWN):
            block = slot * OWN + i
            for t in range(2):
                rows = slice((2 * i + t) * R, (2 * i + t + 1) * R)
                hi, lo = split(agbuf[slot, rows].astype(F32) * scale)
                st[block, :R, t * R : (t + 1) * R] = hi
                st[block, R:, t * R : (t + 1) * R] = lo
            both = st[block]
            out = lax.dot_general(
                both, both, (((1,), (1,)), ((), ())), preferred_element_type=F32
            )
            gram[block] = (out[:R, :R] + out[R:, R:]) + (out[:R, R:] + out[R:, :R])

    def gather_body(step, carry):
        @pl.when((step >= 1) & (step < CHIPS))
        def _():
            ag_copy(step, chip_from(step) * 2 + core).wait_recv()

        @pl.when(step < CHIPS)
        def _():
            fw_copy(step).start()
            take(chip_from(step) * 2 + core)

        @pl.when(step >= 1)
        def _():
            last = step - 1
            fw_copy(last, 1 - core).wait_recv()
            take(chip_from(last) * 2 + 1 - core)

        return carry

    lax.fori_loop(0, CHIPS + 1, gather_body, 0)

    h = h_ref[...]
    eye = eye_mask()
    unit = jnp.where(eye, 1.0, 0.0)

    def first_body(k, start):
        count = count_ref[0, k]
        s = gram[jnp.minimum(start, SLOTS - 1)]
        for i in range(1, MAXB):
            s = s + jnp.where(i < count, gram[jnp.minimum(start + i, SLOTS - 1)], 0.0)
        left = h * w_ref[pl.ds(k, 1), :]
        g = mm_nt(mm(left, s), left)
        square = jnp.sum(jnp.sum(jnp.where(eye, g, 0.0), axis=0, keepdims=True), axis=1, keepdims=True)
        inv_norm = lax.rsqrt(square + 1e-6)
        g = g * (inv_norm * inv_norm)
        gs[k] = g
        qs[k] = unit * inv_norm
        return start + count

    lax.fori_loop(0, RUN_DEV, first_body, jnp.int32(0))

    def newton_body(i, carry):
        def group(j, inner):
            for u in range(4):
                k = j * 4 + u
                g = gs[k]
                c = 1.5 * unit - 0.5 * g
                out = mm(jnp.concatenate([g, qs[k]], axis=0), c)
                qs[k] = out[R:]
                gs[k] = mm(out[:R], c)
            return inner

        return lax.fori_loop(0, RUN_DEV // 4, group, carry)

    lax.fori_loop(0, NSTEPS - 1, newton_body, 0)

    def last_body(k, carry):
        c = 1.5 * unit - 0.5 * gs[k]
        left = h * w_ref[pl.ds(k, 1), :]
        ft[k] = stack_left(mm(mm(qs[k], c), left))
        return carry

    lax.fori_loop(0, RUN_DEV, last_body, 0)

    def project_body(block, carry):
        owner = jnp.int32(0)
        end = jnp.int32(0)
        for k in range(RUN_DEV - 1):
            end = end + count_ref[0, k]
            owner = owner + jnp.where(block >= end, 1, 0)
        out = jnp.dot(ft[owner], st[block], preferred_element_type=F32)
        polar = (out[:R] + out[R:]).astype(BF16)
        rows = pl.ds(pl.multiple_of(block * BLOCK, BLOCK), BLOCK)
        zb[block] = jnp.dot(polar, xv[rows, :], preferred_element_type=F32)
        return carry

    lax.fori_loop(0, SLOTS, project_body, 0)

    left_h = stack_left(h.T)
    bpart[...] = jnp.zeros_like(bpart)
    wcols = wt[...]

    def combine_body(k, start):
        count = count_ref[0, k]
        z = zb[jnp.minimum(start, SLOTS - 1)]
        for i in range(1, MAXB):
            z = z + jnp.where(i < count, zb[jnp.minimum(start + i, SLOTS - 1)], 0.0)
        u = wide(left_h, z)
        us[k] = u
        col = jnp.sum(
            jnp.where(lax.broadcasted_iota(jnp.int32, (R, R), 1) == k, wcols, 0.0), axis=1, keepdims=True
        )
        bpart[...] += (u * col).reshape(N_RUN, R // N_RUN, WIDTH)
        return start + count

    lax.fori_loop(0, RUN_DEV, combine_body, jnp.int32(0))

    def b1_copy(step):
        return send(
            bpart.at[lax.rem(run + step, N_RUN)], brecv.at[step], b1_s.at[step], b1_r.at[step], run_peer(step)
        )

    def b2_copy(step, slot=run):
        return send(ball.at[slot], ball.at[slot], b2_s.at[step], b2_r.at[step], run_peer(step))

    for step in range(1, N_RUN):
        b1_copy(step).start()
    own = bpart[run]
    for step in range(1, N_RUN):
        b1_copy(step).wait_recv()
        own = own + brecv[step]
    ball[run] = own
    for step in range(1, N_RUN):
        b2_copy(step).start()
    for step in range(1, N_RUN):
        b2_copy(step, run_from(step)).wait_recv()

    nmt = wide(stack_left(cinv[...]), ball[...].reshape(R, WIDTH))
    nmt_ref[...] = nmt

    e_part[:R] = self_gram(nmt)
    columns = jnp.zeros((R, R), F32)
    lanes = lax.broadcasted_iota(jnp.int32, (R, R), 1)
    for k in range(RUN_DEV):
        col = jnp.sum(us[k] * nmt, axis=1, keepdims=True)
        columns = jnp.where(lanes == k, col, columns)
    e_part[R:] = columns.T[:16]

    HALF = (R + 16) // 2
    e1 = send(e_part, e_sib, e1_s, e1_r, sibling)
    e1.start()
    e1.wait_recv()
    mine = pl.ds(pl.multiple_of(core * HALF, 8), HALF)
    e_half[...] = e_part[mine] + e_sib[mine]

    def e2_copy(step, slot=chip):
        return send(e_half, e_recv.at[slot], e2_s.at[step], e2_r.at[step], peer(step))

    for step in range(1, CHIPS):
        e2_copy(step).start()
    e_recv[chip] = e_half[...]
    for step in range(1, CHIPS):
        e2_copy(step, chip_from(step)).wait_recv()
    e_out[...] = jnp.sum(e_recv[...], axis=0)
    e3 = send(e_out, e_fin, e3_s, e3_r, sibling)
    e3.start()
    sums_ref[mine] = e_out[...]
    e3.wait_recv()
    other = pl.ds(pl.multiple_of((1 - core) * HALF, 8), HALF)
    sums_ref[other] = e_fin[...]

    for step in range(1, N_RUN):
        w_copy(step).wait_send()
        b1_copy(step).wait_send()
        b2_copy(step).wait_send()
    for step in range(1, CHIPS):
        rs_copy(step - 1).wait_send()
        ag_copy(step).wait_send()
        e2_copy(step).wait_send()
    for step in range(CHIPS):
        d_copy(step).wait_send()
        fw_copy(step).wait_send()
    e1.wait_send()
    e3.wait_send()


def last_kernel(nmt_ref, sums_ref, h_ref, nm_ref, nw_ref):
    nm_ref[...] = nmt_ref[...].T
    h = h_ref[...]
    matrix = sums_ref[:R] * mm(h.T, h)
    scaled, row, column, x, r = inverse_start(matrix)

    def more(carry):
        step, x, r = carry
        return (step < 10) & (jnp.max(jnp.abs(r)) > 1e-6)

    def body(carry):
        step, x, r = carry
        for _ in range(4):
            x, r = inverse_step(x, r)
        return step + 1, x, r

    _, x, r = lax.while_loop(more, body, (jnp.int32(0), x, r))
    x = inverse_polish(scaled, x)
    nw_ref[...] = mm(sums_ref[R:], x * row * column)[:RUN_DEV]


def per_device(spectra, mz_factor, mixing, run_weights, block_count, trim_scans):
    vmem = pl.BlockSpec(memory_space=pltpu.VMEM)
    smem = pl.BlockSpec(memory_space=pltpu.SMEM)
    dma8 = pltpu.SemaphoreType.DMA((8,))
    dma = pltpu.SemaphoreType.DMA
    half = (R + 16) // 2
    nmt, sums = pl.pallas_call(
        main_kernel,
        out_shape=(
            jax.ShapeDtypeStruct((R, WIDTH), F32),
            jax.ShapeDtypeStruct((R + 16, R), F32),
        ),
        in_specs=[pl.BlockSpec(memory_space=pl.ANY), vmem, vmem, vmem, smem, smem],
        out_specs=(vmem, vmem),
        scratch_shapes=[
            pltpu.VMEM((SLOTS * BLOCK, WIDTH), BF16),
            pltpu.VMEM((R, WIDTH), BF16),
            pltpu.VMEM((CHIPS, TILES, R, R), F32),
            pltpu.VMEM((CHIPS, TILES, R, R), F32),
            pltpu.VMEM((CHIPS, TILES, R, R), F32),
            pltpu.VMEM((CHIPS - 1, CODED, R), jnp.int16),
            pltpu.VMEM((CHIPS - 1, CODED, R), jnp.int16),
            pltpu.VMEM((TILES, R, R), F32),
            pltpu.VMEM((2 * CHIPS, CODED, R), jnp.int16),
            pltpu.VMEM((SLOTS, 2 * R, BLOCK), BF16),
            pltpu.VMEM((SLOTS, R, R), F32),
            pltpu.VMEM((RUN_DEV, R, R), F32),
            pltpu.VMEM((RUN_DEV, R, R), F32),
            pltpu.VMEM((RUN_DEV, 2 * R, 2 * R), BF16),
            pltpu.VMEM((SLOTS, R, WIDTH), F32),
            pltpu.VMEM((RUN_DEV, R, WIDTH), F32),
            pltpu.VMEM((N_RUN, 16, R), F32),
            pltpu.VMEM((R, R), F32),
            pltpu.VMEM((R, R), F32),
            pltpu.VMEM((N_RUN, R // N_RUN, WIDTH), F32),
            pltpu.VMEM((N_RUN, R // N_RUN, WIDTH), F32),
            pltpu.VMEM((N_RUN, R // N_RUN, WIDTH), F32),
            pltpu.VMEM((R + 16, R), F32),
            pltpu.VMEM((R + 16, R), F32),
            pltpu.VMEM((half, R), F32),
            pltpu.VMEM((CHIPS, half, R), F32),
            pltpu.VMEM((half, R), F32),
            pltpu.VMEM((half, R), F32),
            dma((2 * CHIPS,)),
            dma8, dma8, dma8, dma8, dma8, dma8, dma8, dma8,
            dma8, dma8, dma8, dma8, dma8, dma8,
            dma, dma, dma8, dma8, dma, dma,
        ],
        compiler_params=pltpu.CompilerParams(
            collective_id=0, has_side_effects=True, vmem_limit_bytes=58 * 2**20
        ),
    )(spectra, mz_factor, mixing, run_weights, block_count, trim_scans)
    return pl.pallas_call(
        last_kernel,
        out_shape=(
            jax.ShapeDtypeStruct((WIDTH, R), F32),
            jax.ShapeDtypeStruct((RUN_DEV, R), F32),
        ),
        in_specs=[vmem, vmem, vmem],
        out_specs=(vmem, vmem),
    )(nmt, sums, mixing)


def solution(mesh):
    placed = (P("run", "mz"), P("mz", None), P(), P("run", None), P("run", None), P("run", None))
    return jax.shard_map(
        per_device,
        mesh=mesh,
        in_specs=placed,
        out_specs=(P("mz", None), P("run", None)),
        check_vma=False,
    )
```

```python
import functools

import jax
import jax.numpy as jnp
from jax import lax
from jax.experimental import pallas as pl
from jax.experimental.pallas import tpu as pltpu
from jax.sharding import PartitionSpec as P

R = 128
BLOCK = 256
NSTEPS = 8
RUN_DEV = 12
SLOTS = 48
MAXB = 8
CHIPS = 8
N_RUN = 8
OWN = 3
PIECES = CHIPS * OWN
PIECE = BLOCK
CODED = PIECE + 16
WIDTH = 256
LEVELS = 32000.0
INV_STEPS = (4, 11, 11)

PAIR_RUNS = RUN_DEV // 2

OFFSETS = ((1, 0), (3, 0), (0, 1), (2, 0), (1, 1), (3, 1), (2, 1))

MESH = pl.DeviceIdType.MESH
F32 = jnp.float32
BF16 = jnp.bfloat16


def split(x):
    hi = x.astype(BF16)
    return hi, (x - hi.astype(F32)).astype(BF16)


def right_of(y):
    yh, yl = split(y)
    right = jnp.concatenate([yh, yl], axis=1)
    return jnp.concatenate([right, right], axis=0)


def times(x, right):
    xh, xl = split(x)
    out = jnp.dot(jnp.concatenate([xh, xl], axis=1), right, preferred_element_type=F32)
    return out[:, :R] + out[:, R:]


def mm(x, y):
    return times(x, right_of(y))


def mm_nt(x, y):
    xh, xl = split(x)
    yh, yl = split(y)
    right = jnp.concatenate(
        [jnp.concatenate([yh, yh], axis=1), jnp.concatenate([yl, yl], axis=1)], axis=0
    )
    out = lax.dot_general(
        jnp.concatenate([xh, xl], axis=1),
        right,
        (((1,), (1,)), ((), ())),
        preferred_element_type=F32,
    )
    return out[:, :R] + out[:, R:]


def stack_left(x):
    xh, xl = split(x)
    return jnp.concatenate(
        [jnp.concatenate([xh, xh], axis=1), jnp.concatenate([xl, xl], axis=1)], axis=0
    )


def wide(left, y):
    yh, yl = split(y)
    out = jnp.dot(left, jnp.concatenate([yh, yl], axis=0), preferred_element_type=F32)
    return out[:R] + out[R:]


def self_gram(x):
    xh, xl = split(x)
    both = jnp.concatenate([xh, xl], axis=0)
    out = lax.dot_general(both, both, (((1,), (1,)), ((), ())), preferred_element_type=F32)
    return out[:R, :R] + out[:R, R:] + out[R:, :R] + out[R:, R:]


def eye_mask():
    return lax.broadcasted_iota(jnp.int32, (R, R), 0) == lax.broadcasted_iota(jnp.int32, (R, R), 1)


def inverse_start(matrix):
    eye = eye_mask()
    diagonal = jnp.where(eye, matrix, 0.0)
    row = lax.rsqrt(jnp.sum(diagonal, axis=0, keepdims=True))
    column = lax.rsqrt(jnp.sum(diagonal, axis=1, keepdims=True))
    scaled = matrix * row * column
    bound = jnp.max(jnp.sum(jnp.abs(scaled), axis=0, keepdims=True), axis=1, keepdims=True)
    alpha = 1.0 / bound
    unit = jnp.where(eye, 1.0, 0.0)
    return scaled, row, column, alpha * unit, unit - alpha * scaled


def inverse_step(x, r):
    out = mm(jnp.concatenate([x, r], axis=0), r)
    return x + out[:R], out[R:]


def inverse_polish(scaled, x):
    residual = jnp.where(eye_mask(), 1.0, 0.0) - mm(scaled, x)
    return x + mm(x, residual)


def encode(x, dst):
    top = jnp.max(jnp.abs(x), axis=0, keepdims=True)
    code = jnp.ceil(jnp.log(jnp.maximum(top, 1e-30)) * 64.0)
    factor = jnp.exp(code * (-1.0 / 64.0)) * LEVELS
    dst[:PIECE] = jnp.round(x * factor).astype(jnp.int32).astype(jnp.int16)
    dst[PIECE:] = jnp.broadcast_to(code, (16, R)).astype(jnp.int32).astype(jnp.int16)


def decode(src):
    scale = decode_scale(src[PIECE:])
    return src[:PIECE].astype(F32) * scale


def decode_scale(code_rows):
    return jnp.exp(code_rows.astype(F32)[:1] * (1.0 / 64.0)) * (1.0 / LEVELS)


def main_kernel(
    x_hbm, v_ref, h_ref, w_ref, count_ref, trim_ref,
    nmt_ref, sums_ref,
    xv, dsend, drecv, keep, rs_send, rs_recv, acc, agbuf, st, gram, gs, qs, f_own, f_sib, ft, zb, us,
    wall, cinv, wt, bpart, brecv, ball, e_part, e_sib, e_half, e_recv, e_out, e_fin,
    xsem, d_s, d_r, rs_s, rs_r, ag_s, ag_r, fw_s, fw_r, w_s, w_r, b1_s, b1_r, b2_s, b2_r,
    e1_s, e1_r, e2_s, e2_r, e3_s, e3_r, f_s, f_r,
):
    run = lax.axis_index("run")
    me = lax.axis_index("mz")
    chip = lax.div(me, 2)
    core = lax.rem(me, 2)
    sibling = (run, chip * 2 + 1 - core)

    def chip_at(step):
        return lax.rem(chip + step, CHIPS)

    def peer(step):
        return (run, chip_at(step) * 2 + core)

    def run_peer(step):
        return (lax.rem(run + step, N_RUN), me)

    def x_chunk(step, side):
        return chip_at(step + 1) * 2 + (core if side else 1 - core)

    def x_copy(step, side):
        rows = pl.ds(pl.multiple_of(x_chunk(step, side) * OWN * BLOCK, BLOCK), OWN * BLOCK)
        return pltpu.make_async_copy(x_hbm.at[rows], xv.at[rows], xsem.at[step * 2 + side])

    for step in range(CHIPS):
        x_copy(step, 0).start()
        x_copy(step, 1).start()

    barrier = pltpu.get_barrier_semaphore()
    pl.semaphore_signal(barrier, inc=1, device_id=sibling, device_id_type=MESH)
    for step in range(1, CHIPS):
        pl.semaphore_signal(barrier, inc=1, device_id=peer(step), device_id_type=MESH)
        pl.semaphore_signal(barrier, inc=1, device_id=run_peer(step), device_id_type=MESH)

    weights = jnp.concatenate([w_ref[...], jnp.zeros((16 - RUN_DEV, R), F32)], axis=0)
    wall[run] = weights

    def partial_body(step, carry):
        x_copy(step, 0).wait()
        x_copy(step, 1).wait()
        for i in range(OWN):
            t = i * CHIPS + step
            outs = []
            for side in range(2):
                first = pl.multiple_of((x_chunk(step, side) * OWN + i) * BLOCK, BLOCK)
                outs.append(
                    jnp.dot(xv[pl.ds(first, BLOCK), :], v_ref[...], preferred_element_type=F32)
                )
            encode(outs[0], dsend.at[t])
            keep[t] = outs[1]
        return carry

    lax.fori_loop(0, CHIPS, partial_body, 0)

    pl.semaphore_wait(barrier, 2 * CHIPS - 1)

    def send(src, dst, s_sem, r_sem, device):
        return pltpu.make_async_remote_copy(
            src_ref=src, dst_ref=dst, send_sem=s_sem, recv_sem=r_sem,
            device_id=device, device_id_type=MESH,
        )

    def run_from(step):
        return lax.rem(run + N_RUN - step, N_RUN)

    def chip_from(step):
        return lax.rem(chip + CHIPS - step, CHIPS)

    def w_copy(step, slot=run):
        return send(wall.at[slot], wall.at[slot], w_s.at[step], w_r.at[step], run_peer(step))

    def d_copy(t):
        return send(dsend.at[t], drecv.at[t], d_s.at[t], d_r.at[t], sibling)

    def rs_copy(t):
        return send(rs_send.at[t], rs_recv.at[t], rs_s.at[t], rs_r.at[t], peer(lax.rem(t, CHIPS) + 1))

    def d_body(t, carry):
        d_copy(t).start()
        return carry

    lax.fori_loop(0, PIECES, d_body, 0)

    def reduce_body(b, carry):
        first = b * CHIPS
        for i in range(CHIPS):
            d_copy(first + i).wait_recv()
        for i in range(CHIPS - 1):
            t = first + i
            encode(keep[t] + decode(drecv.at[t]), rs_send.at[t])
        for i in range(CHIPS - 1):
            rs_copy(first + i).start()
        t = first + CHIPS - 1
        acc[b] = keep[t] + decode(drecv.at[t])
        return carry

    lax.fori_loop(0, OWN, reduce_body, 0)

    for step in range(1, N_RUN):
        w_copy(step).start()

    for step in range(1, N_RUN):
        w_copy(step, run_from(step)).wait_recv()
    all_weights = wall[...].reshape(N_RUN * 16, R)
    h = h_ref[...]
    ht = h.T
    mix_gram = mm(ht, h)
    c_matrix = mm(all_weights.T, all_weights) * mix_gram
    scaled, row, column, x0, r0 = inverse_start(c_matrix)

    def inv_body(i, carry):
        return inverse_step(*carry)

    own_weights = jnp.concatenate([weights, jnp.zeros((R - 16, R), F32)], axis=0)
    wt[...] = own_weights.T

    starts = []
    total = jnp.int32(0)
    for k in range(RUN_DEV):
        starts.append(total)
        total = total + count_ref[0, k]
    ends = starts[1:] + [total]
    scans = lax.broadcasted_iota(jnp.int32, (BLOCK, R), 0)

    def shifted(offset, sign):
        dz, dx = offset
        z = lax.rem(lax.div(chip, 2) + 4 + sign * dz, 4)
        return z * 2 + lax.rem(lax.rem(chip, 2) + dx, 2)

    def ag_copy(i, b, slot=me):
        device = (run, shifted(OFFSETS[i], 1) * 2 + core)
        part = agbuf.at[slot, b]
        return send(part, part, ag_s.at[i * OWN + b], ag_r.at[i * OWN + b], device)

    def source(i):
        return chip if i == CHIPS - 1 else shifted(OFFSETS[i], -1)

    def fw_copy(i, b, side=core):
        part = agbuf.at[source(i) * 2 + side, b]
        return send(part, part, fw_s.at[i * OWN + b], fw_r.at[i * OWN + b], sibling)

    def unpack(slot, b):
        block = slot * OWN + b
        values = decode(agbuf.at[slot, b])
        hi0, lo0 = split(values[:R])
        hi1, lo1 = split(values[R:])
        both = jnp.concatenate(
            [jnp.concatenate([hi0, hi1], axis=1), jnp.concatenate([lo0, lo1], axis=1)], axis=0
        )
        st[block] = both
        return block, both

    def take_pair(i, b):
        fw_copy(i, b, 1 - core).wait_recv()
        pair = [unpack(source(i) * 2 + side, b) for side in (core, 1 - core)]
        for block, both in pair:
            out = lax.dot_general(both, both, (((1,), (1,)), ((), ())), preferred_element_type=F32)
            gram[block] = (out[:R, :R] + out[R:, R:]) + (out[:R, R:] + out[R:, :R])

    for b in range(OWN):
        x0, r0 = lax.fori_loop(0, INV_STEPS[b], inv_body, (x0, r0))
        if b == OWN - 1:
            x0 = inverse_polish(scaled, x0)
            x0 = inverse_polish(scaled, x0)
            cinv[...] = x0 * row * column
        own = acc[b]
        for i in range(CHIPS - 1):
            rs_copy(b * CHIPS + i).wait_recv()
        for i in range(CHIPS - 1):
            own = own + decode(rs_recv.at[b * CHIPS + i])
        block = me * OWN + b
        limit = jnp.int32(BLOCK)
        for k in range(RUN_DEV):
            limit = limit - jnp.where(block == ends[k] - 1, trim_ref[0, k], 0)
        own = jnp.where(scans < limit, own, 0.0)
        encode(jnp.concatenate([own[:R].T, own[R:].T], axis=0), agbuf.at[me, b])
        for i in range(CHIPS - 1):
            ag_copy(i, b).start()
        fw_copy(CHIPS - 1, b).start()

    late = []
    for b in range(OWN):
        take_pair(CHIPS - 1, b)
    for b in range(OWN):
        for i in range(CHIPS - 1):
            ag_copy(i, b, source(i) * 2 + core).wait_recv()
            fw_copy(i, b).start()
            if late:
                take_pair(*late.pop())
            late.append((i, b))
    take_pair(*late.pop())

    h = h_ref[...]
    eye = eye_mask()
    unit = jnp.where(eye, 1.0, 0.0)

    first_run = core * PAIR_RUNS
    pair_runs = range(PAIR_RUNS)
    lefts, sums = [], []
    for j in pair_runs:
        k = first_run + j
        count = count_ref[0, k]
        start = jnp.int32(0)
        for i in range(RUN_DEV - 1):
            start = start + jnp.where(i < k, count_ref[0, i], 0)
        s = gram[jnp.minimum(start, SLOTS - 1)]
        for i in range(1, MAXB):
            s = s + jnp.where(i < count, gram[jnp.minimum(start + i, SLOTS - 1)], 0.0)
        sums.append(s)
        lefts.append(h * w_ref[pl.ds(k, 1), :])
    halves = [mm(lefts[j], sums[j]) for j in pair_runs]
    grams = [mm_nt(halves[j], lefts[j]) for j in pair_runs]
    for j in pair_runs:
        g = grams[j]
        square = jnp.sum(jnp.sum(jnp.where(eye, g, 0.0), axis=0, keepdims=True), axis=1, keepdims=True)
        inv_norm = lax.rsqrt(square + 1e-6)
        gs[j] = g * (inv_norm * inv_norm)
        qs[j] = unit * inv_norm

    def newton_body(i, carry):
        rights = [right_of(1.5 * unit - 0.5 * gs[j]) for j in pair_runs]
        outs = [times(gs[j], rights[j]) for j in pair_runs]
        news = [times(outs[j], rights[j]) for j in pair_runs]
        products = [times(qs[j], rights[j]) for j in pair_runs]
        for j in pair_runs:
            gs[j] = news[j]
            qs[j] = products[j]
        return carry

    lax.fori_loop(0, NSTEPS - 1, newton_body, 0)

    lasts = [mm(qs[j], 1.5 * unit - 0.5 * gs[j]) for j in pair_runs]
    lasts = [mm(lasts[j], h * w_ref[pl.ds(first_run + j, 1), :]) for j in pair_runs]
    for j in pair_runs:
        hi, lo = split(lasts[j])
        f_own[j, :R] = hi
        f_own[j, R:] = lo

    f_copy = send(f_own, f_sib, f_s, f_r, sibling)
    f_copy.start()
    for j in pair_runs:
        ft[first_run + j] = f_own[j]
    f_copy.wait_recv()
    for j in pair_runs:
        ft[PAIR_RUNS - first_run + j] = f_sib[j]

    def project(group):
        polars = []
        for u in range(8):
            block = group * 8 + u
            owner = jnp.int32(0)
            end = jnp.int32(0)
            for k in range(RUN_DEV - 1):
                end = end + count_ref[0, k]
                owner = owner + jnp.where(block >= end, 1, 0)
            factor = ft[owner]
            out = jnp.dot(
                jnp.concatenate([factor, factor], axis=1), st[block], preferred_element_type=F32
            )
            polars.append((out[:R] + out[R:]).astype(BF16))
        for u in range(8):
            block = group * 8 + u
            rows = slice(block * BLOCK, (block + 1) * BLOCK)
            zb[block] = jnp.dot(polars[u], xv[rows, :], preferred_element_type=F32)

    for group in range(SLOTS // 8):
        project(group)

    left_h = stack_left(h.T)
    bpart[...] = jnp.zeros_like(bpart)
    wcols = wt[...]

    def combine_one(k, start):
        count = count_ref[0, k]
        z = zb[jnp.minimum(start, SLOTS - 1)]
        for i in range(1, MAXB):
            z = z + jnp.where(i < count, zb[jnp.minimum(start + i, SLOTS - 1)], 0.0)
        u = wide(left_h, z)
        us[k] = u
        col = jnp.sum(
            jnp.where(lax.broadcasted_iota(jnp.int32, (R, R), 1) == k, wcols, 0.0), axis=1, keepdims=True
        )
        bpart[...] += (u * col).reshape(N_RUN, R // N_RUN, WIDTH)
        return start + count

    start = jnp.int32(0)
    for k in range(RUN_DEV):
        start = combine_one(k, start)

    def b1_copy(step):
        return send(
            bpart.at[lax.rem(run + step, N_RUN)], brecv.at[step], b1_s.at[step], b1_r.at[step], run_peer(step)
        )

    def b2_copy(step, slot=run):
        return send(ball.at[slot], ball.at[slot], b2_s.at[step], b2_r.at[step], run_peer(step))

    for step in range(1, N_RUN):
        b1_copy(step).start()
    own = bpart[run]
    for step in range(1, N_RUN):
        b1_copy(step).wait_recv()
        own = own + brecv[step]
    ball[run] = own
    for step in range(1, N_RUN):
        b2_copy(step).start()
    for step in range(1, N_RUN):
        b2_copy(step, run_from(step)).wait_recv()

    nmt = wide(stack_left(cinv[...]), ball[...].reshape(R, WIDTH))
    nmt_ref[...] = nmt

    e_part[:R] = self_gram(nmt)
    columns = jnp.zeros((R, R), F32)
    lanes = lax.broadcasted_iota(jnp.int32, (R, R), 1)
    for k in range(RUN_DEV):
        col = jnp.sum(us[k] * nmt, axis=1, keepdims=True)
        columns = jnp.where(lanes == k, col, columns)
    e_part[R:] = columns.T[:16]

    HALF = (R + 16) // 2
    e1 = send(e_part, e_sib, e1_s, e1_r, sibling)
    e1.start()
    e1.wait_recv()
    mine = pl.ds(pl.multiple_of(core * HALF, 8), HALF)
    e_half[...] = e_part[mine] + e_sib[mine]

    def e2_copy(step, slot=chip):
        return send(e_half, e_recv.at[slot], e2_s.at[step], e2_r.at[step], peer(step))

    for step in range(1, CHIPS):
        e2_copy(step).start()
    e_recv[chip] = e_half[...]
    for step in range(1, CHIPS):
        e2_copy(step, chip_from(step)).wait_recv()
    e_out[...] = jnp.sum(e_recv[...], axis=0)
    e3 = send(e_out, e_fin, e3_s, e3_r, sibling)
    e3.start()
    sums_ref[mine] = e_out[...]
    e3.wait_recv()
    other = pl.ds(pl.multiple_of((1 - core) * HALF, 8), HALF)
    sums_ref[other] = e_fin[...]

    for step in range(1, N_RUN):
        w_copy(step).wait_send()
        b1_copy(step).wait_send()
        b2_copy(step).wait_send()
    for i in range(CHIPS - 1):
        e2_copy(i + 1).wait_send()
        for b in range(OWN):
            rs_copy(b * CHIPS + i).wait_send()
            ag_copy(i, b).wait_send()
    for i in range(CHIPS):
        for b in range(OWN):
            d_copy(b * CHIPS + i).wait_send()
            fw_copy(i, b).wait_send()
    e1.wait_send()
    e3.wait_send()
    f_copy.wait_send()


def last_kernel(nmt_ref, sums_ref, h_ref, nm_ref, nw_ref):
    nm_ref[...] = nmt_ref[...].T
    h = h_ref[...]
    matrix = sums_ref[:R] * mm(h.T, h)
    scaled, row, column, x, r = inverse_start(matrix)

    def more(carry):
        step, x, r = carry
        return (step < 10) & (jnp.max(jnp.abs(r)) > 1e-6)

    def body(carry):
        step, x, r = carry
        for _ in range(4):
            x, r = inverse_step(x, r)
        return step + 1, x, r

    _, x, r = lax.while_loop(more, body, (jnp.int32(0), x, r))
    x = inverse_polish(scaled, x)
    nw_ref[...] = mm(sums_ref[R:], x * row * column)[:RUN_DEV]


def per_device(spectra, mz_factor, mixing, run_weights, block_count, trim_scans):
    vmem = pl.BlockSpec(memory_space=pltpu.VMEM)
    smem = pl.BlockSpec(memory_space=pltpu.SMEM)
    dma8 = pltpu.SemaphoreType.DMA((8,))
    dma = pltpu.SemaphoreType.DMA
    half = (R + 16) // 2
    nmt, sums = pl.pallas_call(
        main_kernel,
        out_shape=(
            jax.ShapeDtypeStruct((R, WIDTH), F32),
            jax.ShapeDtypeStruct((R + 16, R), F32),
        ),
        in_specs=[pl.BlockSpec(memory_space=pl.ANY), vmem, vmem, vmem, smem, smem],
        out_specs=(vmem, vmem),
        scratch_shapes=[
            pltpu.VMEM((SLOTS * BLOCK, WIDTH), BF16),
            pltpu.VMEM((PIECES, CODED, R), jnp.int16),
            pltpu.VMEM((PIECES, CODED, R), jnp.int16),
            pltpu.VMEM((PIECES, BLOCK, R), F32),
            pltpu.VMEM((PIECES, CODED, R), jnp.int16),
            pltpu.VMEM((PIECES, CODED, R), jnp.int16),
            pltpu.VMEM((OWN, BLOCK, R), F32),
            pltpu.VMEM((2 * CHIPS, OWN, CODED, R), jnp.int16),
            pltpu.VMEM((SLOTS, 2 * R, BLOCK), BF16),
            pltpu.VMEM((SLOTS, R, R), F32),
            pltpu.VMEM((PAIR_RUNS, R, R), F32),
            pltpu.VMEM((PAIR_RUNS, R, R), F32),
            pltpu.VMEM((PAIR_RUNS, 2 * R, R), BF16),
            pltpu.VMEM((PAIR_RUNS, 2 * R, R), BF16),
            pltpu.VMEM((RUN_DEV, 2 * R, R), BF16),
            pltpu.VMEM((SLOTS, R, WIDTH), F32),
            pltpu.VMEM((RUN_DEV, R, WIDTH), F32),
            pltpu.VMEM((N_RUN, 16, R), F32),
            pltpu.VMEM((R, R), F32),
            pltpu.VMEM((R, R), F32),
            pltpu.VMEM((N_RUN, R // N_RUN, WIDTH), F32),
            pltpu.VMEM((N_RUN, R // N_RUN, WIDTH), F32),
            pltpu.VMEM((N_RUN, R // N_RUN, WIDTH), F32),
            pltpu.VMEM((R + 16, R), F32),
            pltpu.VMEM((R + 16, R), F32),
            pltpu.VMEM((half, R), F32),
            pltpu.VMEM((CHIPS, half, R), F32),
            pltpu.VMEM((half, R), F32),
            pltpu.VMEM((half, R), F32),
            dma((2 * CHIPS,)),
            dma((PIECES,)), dma((PIECES,)), dma((PIECES,)), dma((PIECES,)),
            dma((PIECES,)), dma((PIECES,)), dma((PIECES,)), dma((PIECES,)),
            dma8, dma8, dma8, dma8, dma8, dma8,
            dma, dma, dma8, dma8, dma, dma, dma, dma,
        ],
        compiler_params=pltpu.CompilerParams(
            collective_id=0, has_side_effects=True, vmem_limit_bytes=58 * 2**20
        ),
    )(spectra, mz_factor, mixing, run_weights, block_count, trim_scans)
    return pl.pallas_call(
        last_kernel,
        out_shape=(
            jax.ShapeDtypeStruct((WIDTH, R), F32),
            jax.ShapeDtypeStruct((RUN_DEV, R), F32),
        ),
        in_specs=[vmem, vmem, vmem],
        out_specs=(vmem, vmem),
    )(nmt, sums, mixing)


def solution(mesh):
    placed = (P("run", "mz"), P("mz", None), P(), P("run", None), P("run", None), P("run", None))
    return jax.shard_map(
        per_device,
        mesh=mesh,
        in_specs=placed,
        out_specs=(P("mz", None), P("run", None)),
        check_vma=False,
    )
```

```python
import functools

import jax
import jax.numpy as jnp
from jax import lax
from jax.experimental import pallas as pl
from jax.experimental.pallas import tpu as pltpu
from jax.sharding import PartitionSpec as P

R = 128
BLOCK = 256
NSTEPS = 8
RUN_DEV = 12
SLOTS = 48
MAXB = 8
CHIPS = 8
N_RUN = 8
OWN = 3
PIECES = CHIPS * OWN
PIECE = BLOCK
CODED = PIECE + 16
WIDTH = 256
LEVELS = 32000.0
INV_STEPS = (4, 11, 11)

PAIR_RUNS = RUN_DEV // 2

OFFSETS = ((1, 0), (3, 0), (0, 1), (2, 0), (1, 1), (3, 1), (2, 1))

MESH = pl.DeviceIdType.MESH
F32 = jnp.float32
BF16 = jnp.bfloat16


def split(x):
    hi = x.astype(BF16)
    return hi, (x - hi.astype(F32)).astype(BF16)


def right_of(y):
    yh, yl = split(y)
    right = jnp.concatenate([yh, yl], axis=1)
    return jnp.concatenate([right, right], axis=0)


def times(x, right):
    xh, xl = split(x)
    out = jnp.dot(jnp.concatenate([xh, xl], axis=1), right, preferred_element_type=F32)
    return out[:, :R] + out[:, R:]


def mm(x, y):
    return times(x, right_of(y))


def mm_nt(x, y):
    xh, xl = split(x)
    yh, yl = split(y)
    right = jnp.concatenate(
        [jnp.concatenate([yh, yh], axis=1), jnp.concatenate([yl, yl], axis=1)], axis=0
    )
    out = lax.dot_general(
        jnp.concatenate([xh, xl], axis=1),
        right,
        (((1,), (1,)), ((), ())),
        preferred_element_type=F32,
    )
    return out[:, :R] + out[:, R:]


def stack_left(x):
    xh, xl = split(x)
    return jnp.concatenate(
        [jnp.concatenate([xh, xh], axis=1), jnp.concatenate([xl, xl], axis=1)], axis=0
    )


def wide(left, y):
    yh, yl = split(y)
    out = jnp.dot(left, jnp.concatenate([yh, yl], axis=0), preferred_element_type=F32)
    return out[:R] + out[R:]


def self_gram(x):
    xh, xl = split(x)
    both = jnp.concatenate([xh, xl], axis=0)
    out = lax.dot_general(both, both, (((1,), (1,)), ((), ())), preferred_element_type=F32)
    return out[:R, :R] + out[:R, R:] + out[R:, :R] + out[R:, R:]


def eye_mask():
    return lax.broadcasted_iota(jnp.int32, (R, R), 0) == lax.broadcasted_iota(jnp.int32, (R, R), 1)


def inverse_start(matrix):
    eye = eye_mask()
    diagonal = jnp.where(eye, matrix, 0.0)
    row = lax.rsqrt(jnp.sum(diagonal, axis=0, keepdims=True))
    column = lax.rsqrt(jnp.sum(diagonal, axis=1, keepdims=True))
    scaled = matrix * row * column
    bound = jnp.max(jnp.sum(jnp.abs(scaled), axis=0, keepdims=True), axis=1, keepdims=True)
    alpha = 1.0 / bound
    unit = jnp.where(eye, 1.0, 0.0)
    return scaled, row, column, alpha * unit, unit - alpha * scaled


def inverse_step(x, r):
    out = mm(jnp.concatenate([x, r], axis=0), r)
    return x + out[:R], out[R:]


def inverse_polish(scaled, x):
    residual = jnp.where(eye_mask(), 1.0, 0.0) - mm(scaled, x)
    return x + mm(x, residual)


def encode(x, dst):
    top = jnp.max(jnp.abs(x), axis=0, keepdims=True)
    code = jnp.ceil(jnp.log(jnp.maximum(top, 1e-30)) * 64.0)
    factor = jnp.exp(code * (-1.0 / 64.0)) * LEVELS
    dst[:PIECE] = jnp.round(x * factor).astype(jnp.int32).astype(jnp.int16)
    dst[PIECE:] = jnp.broadcast_to(code, (16, R)).astype(jnp.int32).astype(jnp.int16)


def decode(src):
    scale = decode_scale(src[PIECE:])
    return src[:PIECE].astype(F32) * scale


def decode_scale(code_rows):
    return jnp.exp(code_rows.astype(F32)[:1] * (1.0 / 64.0)) * (1.0 / LEVELS)


def main_kernel(
    x_hbm, v_ref, h_ref, w_ref, count_ref, trim_ref,
    nmt_ref, sums_ref,
    xv, dsend, drecv, keep, rs_send, rs_recv, acc, agbuf, st, gram, gs, qs, f_own, f_sib, ft, zb, us,
    wall, cinv, wt, bpart, brecv, ball, e_part, e_sib, e_half, e_recv, e_out, e_fin,
    xsem, d_s, d_r, rs_s, rs_r, ag_s, ag_r, fw_s, fw_r, w_s, w_r, b1_s, b1_r, b2_s, b2_r,
    e1_s, e1_r, e2_s, e2_r, e3_s, e3_r, f_s, f_r,
):
    run = lax.axis_index("run")
    me = lax.axis_index("mz")
    chip = lax.div(me, 2)
    core = lax.rem(me, 2)
    sibling = (run, chip * 2 + 1 - core)

    def chip_at(step):
        return lax.rem(chip + step, CHIPS)

    def peer(step):
        return (run, chip_at(step) * 2 + core)

    def run_peer(step):
        return (lax.rem(run + step, N_RUN), me)

    def x_chunk(step, side):
        return chip_at(step + 1) * 2 + (core if side else 1 - core)

    def x_copy(step, side):
        rows = pl.ds(pl.multiple_of(x_chunk(step, side) * OWN * BLOCK, BLOCK), OWN * BLOCK)
        return pltpu.make_async_copy(x_hbm.at[rows], xv.at[rows], xsem.at[step * 2 + side])

    for step in range(CHIPS):
        x_copy(step, 0).start()
        x_copy(step, 1).start()

    barrier = pltpu.get_barrier_semaphore()
    pl.semaphore_signal(barrier, inc=1, device_id=sibling, device_id_type=MESH)
    for step in range(1, CHIPS):
        pl.semaphore_signal(barrier, inc=1, device_id=peer(step), device_id_type=MESH)
        pl.semaphore_signal(barrier, inc=1, device_id=run_peer(step), device_id_type=MESH)

    weights = jnp.concatenate([w_ref[...], jnp.zeros((16 - RUN_DEV, R), F32)], axis=0)
    wall[run] = weights

    def partial_body(step, carry):
        x_copy(step, 0).wait()
        x_copy(step, 1).wait()
        for i in range(OWN):
            t = i * CHIPS + step
            outs = []
            for side in range(2):
                first = pl.multiple_of((x_chunk(step, side) * OWN + i) * BLOCK, BLOCK)
                outs.append(
                    jnp.dot(xv[pl.ds(first, BLOCK), :], v_ref[...], preferred_element_type=F32)
                )
            encode(outs[0], dsend.at[t])
            keep[t] = outs[1]
        return carry

    lax.fori_loop(0, CHIPS, partial_body, 0)

    pl.semaphore_wait(barrier, 2 * CHIPS - 1)

    def send(src, dst, s_sem, r_sem, device):
        return pltpu.make_async_remote_copy(
            src_ref=src, dst_ref=dst, send_sem=s_sem, recv_sem=r_sem,
            device_id=device, device_id_type=MESH,
        )

    def run_from(step):
        return lax.rem(run + N_RUN - step, N_RUN)

    def chip_from(step):
        return lax.rem(chip + CHIPS - step, CHIPS)

    def w_copy(step, slot=run):
        return send(wall.at[slot], wall.at[slot], w_s.at[step], w_r.at[step], run_peer(step))

    def d_copy(t):
        return send(dsend.at[t], drecv.at[t], d_s.at[t], d_r.at[t], sibling)

    def rs_copy(t):
        return send(rs_send.at[t], rs_recv.at[t], rs_s.at[t], rs_r.at[t], peer(lax.rem(t, CHIPS) + 1))

    def d_start(b):
        for i in range(CHIPS):
            d_copy(b * CHIPS + i).start()

    def rs_encode(b):
        for i in range(CHIPS):
            d_copy(b * CHIPS + i).wait_recv()
        for i in range(CHIPS - 1):
            t = b * CHIPS + i
            encode(keep[t] + decode(drecv.at[t]), rs_send.at[t])
        t = b * CHIPS + CHIPS - 1
        acc[b] = keep[t] + decode(drecv.at[t])

    def rs_start(b):
        for i in range(CHIPS - 1):
            rs_copy(b * CHIPS + i).start()

    d_start(0)
    for step in range(1, N_RUN):
        w_copy(step).start()
    rs_encode(0)
    d_start(1)
    rs_start(0)
    d_start(2)
    rs_encode(1)

    for step in range(1, N_RUN):
        w_copy(step, run_from(step)).wait_recv()
    all_weights = wall[...].reshape(N_RUN * 16, R)
    h = h_ref[...]
    ht = h.T
    mix_gram = mm(ht, h)
    c_matrix = mm(all_weights.T, all_weights) * mix_gram
    scaled, row, column, x0, r0 = inverse_start(c_matrix)

    def inv_body(i, carry):
        return inverse_step(*carry)

    x0, r0 = lax.fori_loop(0, INV_STEPS[0], inv_body, (x0, r0))
    rs_start(1)
    rs_encode(2)
    x0, r0 = lax.fori_loop(0, INV_STEPS[1], inv_body, (x0, r0))
    rs_start(2)
    x0, r0 = lax.fori_loop(0, INV_STEPS[2], inv_body, (x0, r0))
    x0 = inverse_polish(scaled, x0)
    x0 = inverse_polish(scaled, x0)
    cinv[...] = x0 * row * column
    own_weights = jnp.concatenate([weights, jnp.zeros((R - 16, R), F32)], axis=0)
    wt[...] = own_weights.T

    starts = []
    total = jnp.int32(0)
    for k in range(RUN_DEV):
        starts.append(total)
        total = total + count_ref[0, k]
    ends = starts[1:] + [total]
    scans = lax.broadcasted_iota(jnp.int32, (BLOCK, R), 0)

    def shifted(offset, sign):
        dz, dx = offset
        z = lax.rem(lax.div(chip, 2) + 4 + sign * dz, 4)
        return z * 2 + lax.rem(lax.rem(chip, 2) + dx, 2)

    def ag_copy(i, b, slot=me):
        device = (run, shifted(OFFSETS[i], 1) * 2 + core)
        part = agbuf.at[slot, b]
        return send(part, part, ag_s.at[i * OWN + b], ag_r.at[i * OWN + b], device)

    def source(i):
        return chip if i == CHIPS - 1 else shifted(OFFSETS[i], -1)

    def fw_copy(i, b, side=core):
        part = agbuf.at[source(i) * 2 + side, b]
        return send(part, part, fw_s.at[i * OWN + b], fw_r.at[i * OWN + b], sibling)

    def unpack(slot, b):
        block = slot * OWN + b
        values = decode(agbuf.at[slot, b])
        hi0, lo0 = split(values[:R])
        hi1, lo1 = split(values[R:])
        both = jnp.concatenate(
            [jnp.concatenate([hi0, hi1], axis=1), jnp.concatenate([lo0, lo1], axis=1)], axis=0
        )
        st[block] = both
        return block, both

    def take_pair(i, b):
        fw_copy(i, b, 1 - core).wait_recv()
        pair = [unpack(source(i) * 2 + side, b) for side in (core, 1 - core)]
        for block, both in pair:
            out = lax.dot_general(both, both, (((1,), (1,)), ((), ())), preferred_element_type=F32)
            gram[block] = (out[:R, :R] + out[R:, R:]) + (out[:R, R:] + out[R:, :R])

    for b in range(OWN):
        own = acc[b]
        for i in range(CHIPS - 1):
            rs_copy(b * CHIPS + i).wait_recv()
        for i in range(CHIPS - 1):
            own = own + decode(rs_recv.at[b * CHIPS + i])
        block = me * OWN + b
        limit = jnp.int32(BLOCK)
        for k in range(RUN_DEV):
            limit = limit - jnp.where(block == ends[k] - 1, trim_ref[0, k], 0)
        own = jnp.where(scans < limit, own, 0.0)
        encode(jnp.concatenate([own[:R].T, own[R:].T], axis=0), agbuf.at[me, b])
        for i in range(CHIPS - 1):
            ag_copy(i, b).start()
        fw_copy(CHIPS - 1, b).start()
        if b:
            take_pair(CHIPS - 1, b - 1)

    take_pair(CHIPS - 1, OWN - 1)
    late = []
    for b in range(OWN):
        for i in range(CHIPS - 1):
            ag_copy(i, b, source(i) * 2 + core).wait_recv()
            fw_copy(i, b).start()
            if late:
                take_pair(*late.pop())
            late.append((i, b))
    take_pair(*late.pop())

    h = h_ref[...]
    eye = eye_mask()
    unit = jnp.where(eye, 1.0, 0.0)

    first_run = core * PAIR_RUNS
    pair_runs = range(PAIR_RUNS)
    lefts, sums = [], []
    for j in pair_runs:
        k = first_run + j
        count = count_ref[0, k]
        start = jnp.int32(0)
        for i in range(RUN_DEV - 1):
            start = start + jnp.where(i < k, count_ref[0, i], 0)
        s = gram[jnp.minimum(start, SLOTS - 1)]
        for i in range(1, MAXB):
            s = s + jnp.where(i < count, gram[jnp.minimum(start + i, SLOTS - 1)], 0.0)
        sums.append(s)
        lefts.append(h * w_ref[pl.ds(k, 1), :])
    halves = [mm(lefts[j], sums[j]) for j in pair_runs]
    grams = [mm_nt(halves[j], lefts[j]) for j in pair_runs]
    for j in pair_runs:
        g = grams[j]
        square = jnp.sum(jnp.sum(jnp.where(eye, g, 0.0), axis=0, keepdims=True), axis=1, keepdims=True)
        inv_norm = lax.rsqrt(square + 1e-6)
        gs[j] = g * (inv_norm * inv_norm)
        qs[j] = unit * inv_norm

    def newton_body(i, carry):
        rights = [right_of(1.5 * unit - 0.5 * gs[j]) for j in pair_runs]
        outs = [times(gs[j], rights[j]) for j in pair_runs]
        news = [times(outs[j], rights[j]) for j in pair_runs]
        products = [times(qs[j], rights[j]) for j in pair_runs]
        for j in pair_runs:
            gs[j] = news[j]
            qs[j] = products[j]
        return carry

    lax.fori_loop(0, NSTEPS - 1, newton_body, 0)

    lasts = [mm(qs[j], 1.5 * unit - 0.5 * gs[j]) for j in pair_runs]
    lasts = [mm(lasts[j], h * w_ref[pl.ds(first_run + j, 1), :]) for j in pair_runs]
    for j in pair_runs:
        hi, lo = split(lasts[j])
        f_own[j, :R] = hi
        f_own[j, R:] = lo

    f_copy = send(f_own, f_sib, f_s, f_r, sibling)
    f_copy.start()
    for j in pair_runs:
        ft[first_run + j] = f_own[j]
    f_copy.wait_recv()
    for j in pair_runs:
        ft[PAIR_RUNS - first_run + j] = f_sib[j]

    def project(group):
        polars = []
        for u in range(8):
            block = group * 8 + u
            owner = jnp.int32(0)
            end = jnp.int32(0)
            for k in range(RUN_DEV - 1):
                end = end + count_ref[0, k]
                owner = owner + jnp.where(block >= end, 1, 0)
            factor = ft[owner]
            out = jnp.dot(
                jnp.concatenate([factor, factor], axis=1), st[block], preferred_element_type=F32
            )
            polars.append((out[:R] + out[R:]).astype(BF16))
        for u in range(8):
            block = group * 8 + u
            rows = slice(block * BLOCK, (block + 1) * BLOCK)
            zb[block] = jnp.dot(polars[u], xv[rows, :], preferred_element_type=F32)

    for group in range(SLOTS // 8):
        project(group)

    left_h = stack_left(h.T)
    bpart[...] = jnp.zeros_like(bpart)
    wcols = wt[...]

    def combine_one(k, start):
        count = count_ref[0, k]
        z = zb[jnp.minimum(start, SLOTS - 1)]
        for i in range(1, MAXB):
            z = z + jnp.where(i < count, zb[jnp.minimum(start + i, SLOTS - 1)], 0.0)
        u = wide(left_h, z)
        us[k] = u
        col = jnp.sum(
            jnp.where(lax.broadcasted_iota(jnp.int32, (R, R), 1) == k, wcols, 0.0), axis=1, keepdims=True
        )
        bpart[...] += (u * col).reshape(N_RUN, R // N_RUN, WIDTH)
        return start + count

    start = jnp.int32(0)
    for k in range(RUN_DEV):
        start = combine_one(k, start)

    def b1_copy(step):
        return send(
            bpart.at[lax.rem(run + step, N_RUN)], brecv.at[step], b1_s.at[step], b1_r.at[step], run_peer(step)
        )

    def b2_copy(step, slot=run):
        return send(ball.at[slot], ball.at[slot], b2_s.at[step], b2_r.at[step], run_peer(step))

    for step in range(1, N_RUN):
        b1_copy(step).start()
    own = bpart[run]
    for step in range(1, N_RUN):
        b1_copy(step).wait_recv()
        own = own + brecv[step]
    ball[run] = own
    for step in range(1, N_RUN):
        b2_copy(step).start()
    for step in range(1, N_RUN):
        b2_copy(step, run_from(step)).wait_recv()

    nmt = wide(stack_left(cinv[...]), ball[...].reshape(R, WIDTH))
    nmt_ref[...] = nmt

    e_part[:R] = self_gram(nmt)
    columns = jnp.zeros((R, R), F32)
    lanes = lax.broadcasted_iota(jnp.int32, (R, R), 1)
    for k in range(RUN_DEV):
        col = jnp.sum(us[k] * nmt, axis=1, keepdims=True)
        columns = jnp.where(lanes == k, col, columns)
    e_part[R:] = columns.T[:16]

    HALF = (R + 16) // 2
    e1 = send(e_part, e_sib, e1_s, e1_r, sibling)
    e1.start()
    e1.wait_recv()
    mine = pl.ds(pl.multiple_of(core * HALF, 8), HALF)
    e_half[...] = e_part[mine] + e_sib[mine]

    def e2_copy(step, slot=chip):
        return send(e_half, e_recv.at[slot], e2_s.at[step], e2_r.at[step], peer(step))

    for step in range(1, CHIPS):
        e2_copy(step).start()
    e_recv[chip] = e_half[...]
    for step in range(1, CHIPS):
        e2_copy(step, chip_from(step)).wait_recv()
    e_out[...] = jnp.sum(e_recv[...], axis=0)
    e3 = send(e_out, e_fin, e3_s, e3_r, sibling)
    e3.start()
    sums_ref[mine] = e_out[...]
    e3.wait_recv()
    other = pl.ds(pl.multiple_of((1 - core) * HALF, 8), HALF)
    sums_ref[other] = e_fin[...]

    for step in range(1, N_RUN):
        w_copy(step).wait_send()
        b1_copy(step).wait_send()
        b2_copy(step).wait_send()
    for i in range(CHIPS - 1):
        e2_copy(i + 1).wait_send()
        for b in range(OWN):
            rs_copy(b * CHIPS + i).wait_send()
            ag_copy(i, b).wait_send()
    for i in range(CHIPS):
        for b in range(OWN):
            d_copy(b * CHIPS + i).wait_send()
            fw_copy(i, b).wait_send()
    e1.wait_send()
    e3.wait_send()
    f_copy.wait_send()


def last_kernel(nmt_ref, sums_ref, h_ref, nm_ref, nw_ref):
    nm_ref[...] = nmt_ref[...].T
    h = h_ref[...]
    matrix = sums_ref[:R] * mm(h.T, h)
    scaled, row, column, x, r = inverse_start(matrix)

    def more(carry):
        step, x, r = carry
        return (step < 10) & (jnp.max(jnp.abs(r)) > 1e-6)

    def body(carry):
        step, x, r = carry
        for _ in range(4):
            x, r = inverse_step(x, r)
        return step + 1, x, r

    _, x, r = lax.while_loop(more, body, (jnp.int32(0), x, r))
    x = inverse_polish(scaled, x)
    nw_ref[...] = mm(sums_ref[R:], x * row * column)[:RUN_DEV]


def per_device(spectra, mz_factor, mixing, run_weights, block_count, trim_scans):
    vmem = pl.BlockSpec(memory_space=pltpu.VMEM)
    smem = pl.BlockSpec(memory_space=pltpu.SMEM)
    dma8 = pltpu.SemaphoreType.DMA((8,))
    dma = pltpu.SemaphoreType.DMA
    half = (R + 16) // 2
    nmt, sums = pl.pallas_call(
        main_kernel,
        out_shape=(
            jax.ShapeDtypeStruct((R, WIDTH), F32),
            jax.ShapeDtypeStruct((R + 16, R), F32),
        ),
        in_specs=[pl.BlockSpec(memory_space=pl.ANY), vmem, vmem, vmem, smem, smem],
        out_specs=(vmem, vmem),
        scratch_shapes=[
            pltpu.VMEM((SLOTS * BLOCK, WIDTH), BF16),
            pltpu.VMEM((PIECES, CODED, R), jnp.int16),
            pltpu.VMEM((PIECES, CODED, R), jnp.int16),
            pltpu.VMEM((PIECES, BLOCK, R), F32),
            pltpu.VMEM((PIECES, CODED, R), jnp.int16),
            pltpu.VMEM((PIECES, CODED, R), jnp.int16),
            pltpu.VMEM((OWN, BLOCK, R), F32),
            pltpu.VMEM((2 * CHIPS, OWN, CODED, R), jnp.int16),
            pltpu.VMEM((SLOTS, 2 * R, BLOCK), BF16),
            pltpu.VMEM((SLOTS, R, R), F32),
            pltpu.VMEM((PAIR_RUNS, R, R), F32),
            pltpu.VMEM((PAIR_RUNS, R, R), F32),
            pltpu.VMEM((PAIR_RUNS, 2 * R, R), BF16),
            pltpu.VMEM((PAIR_RUNS, 2 * R, R), BF16),
            pltpu.VMEM((RUN_DEV, 2 * R, R), BF16),
            pltpu.VMEM((SLOTS, R, WIDTH), F32),
            pltpu.VMEM((RUN_DEV, R, WIDTH), F32),
            pltpu.VMEM((N_RUN, 16, R), F32),
            pltpu.VMEM((R, R), F32),
            pltpu.VMEM((R, R), F32),
            pltpu.VMEM((N_RUN, R // N_RUN, WIDTH), F32),
            pltpu.VMEM((N_RUN, R // N_RUN, WIDTH), F32),
            pltpu.VMEM((N_RUN, R // N_RUN, WIDTH), F32),
            pltpu.VMEM((R + 16, R), F32),
            pltpu.VMEM((R + 16, R), F32),
            pltpu.VMEM((half, R), F32),
            pltpu.VMEM((CHIPS, half, R), F32),
            pltpu.VMEM((half, R), F32),
            pltpu.VMEM((half, R), F32),
            dma((2 * CHIPS,)),
            dma((PIECES,)), dma((PIECES,)), dma((PIECES,)), dma((PIECES,)),
            dma((PIECES,)), dma((PIECES,)), dma((PIECES,)), dma((PIECES,)),
            dma8, dma8, dma8, dma8, dma8, dma8,
            dma, dma, dma8, dma8, dma, dma, dma, dma,
        ],
        compiler_params=pltpu.CompilerParams(
            collective_id=0, has_side_effects=True, vmem_limit_bytes=58 * 2**20
        ),
    )(spectra, mz_factor, mixing, run_weights, block_count, trim_scans)
    return pl.pallas_call(
        last_kernel,
        out_shape=(
            jax.ShapeDtypeStruct((WIDTH, R), F32),
            jax.ShapeDtypeStruct((RUN_DEV, R), F32),
        ),
        in_specs=[vmem, vmem, vmem],
        out_specs=(vmem, vmem),
    )(nmt, sums, mixing)


def solution(mesh):
    placed = (P("run", "mz"), P("mz", None), P(), P("run", None), P("run", None), P("run", None))
    return jax.shard_map(
        per_device,
        mesh=mesh,
        in_specs=placed,
        out_specs=(P("mz", None), P("run", None)),
        check_vma=False,
    )
```

```python
import functools

import jax
import jax.numpy as jnp
from jax import lax
from jax.experimental import pallas as pl
from jax.experimental.pallas import tpu as pltpu
from jax.sharding import PartitionSpec as P

R = 128
BLOCK = 256
NSTEPS = 8
RUN_DEV = 12
SLOTS = 48
MAXB = 8
CHIPS = 8
N_RUN = 8
OWN = 3
PIECES = CHIPS * OWN
PIECE = BLOCK
CODED = PIECE + 16
WIDTH = 256
LEVELS = 32000.0
INV_STEPS = (4, 11, 11)

PAIR_RUNS = RUN_DEV // 2

OFFSETS = ((1, 0), (3, 0), (0, 1), (2, 0), (1, 1), (3, 1), (2, 1))

FAR_FIRST = (4, 5, 3, 6, 2, 7, 1)

MESH = pl.DeviceIdType.MESH
F32 = jnp.float32
BF16 = jnp.bfloat16


def split(x):
    hi = x.astype(BF16)
    return hi, (x - hi.astype(F32)).astype(BF16)


def right_of(y):
    yh, yl = split(y)
    right = jnp.concatenate([yh, yl], axis=1)
    return jnp.concatenate([right, right], axis=0)


def times(x, right):
    xh, xl = split(x)
    out = jnp.dot(jnp.concatenate([xh, xl], axis=1), right, preferred_element_type=F32)
    return out[:, :R] + out[:, R:]


def mm(x, y):
    return times(x, right_of(y))


def mm_nt(x, y):
    xh, xl = split(x)
    yh, yl = split(y)
    right = jnp.concatenate(
        [jnp.concatenate([yh, yh], axis=1), jnp.concatenate([yl, yl], axis=1)], axis=0
    )
    out = lax.dot_general(
        jnp.concatenate([xh, xl], axis=1),
        right,
        (((1,), (1,)), ((), ())),
        preferred_element_type=F32,
    )
    return out[:, :R] + out[:, R:]


def stack_left(x):
    xh, xl = split(x)
    return jnp.concatenate(
        [jnp.concatenate([xh, xh], axis=1), jnp.concatenate([xl, xl], axis=1)], axis=0
    )


def wide(left, y):
    yh, yl = split(y)
    out = jnp.dot(left, jnp.concatenate([yh, yl], axis=0), preferred_element_type=F32)
    return out[:R] + out[R:]


def self_gram(x):
    xh, xl = split(x)
    both = jnp.concatenate([xh, xl], axis=0)
    out = lax.dot_general(both, both, (((1,), (1,)), ((), ())), preferred_element_type=F32)
    return out[:R, :R] + out[:R, R:] + out[R:, :R] + out[R:, R:]


def eye_mask():
    return lax.broadcasted_iota(jnp.int32, (R, R), 0) == lax.broadcasted_iota(jnp.int32, (R, R), 1)


def inverse_start(matrix):
    eye = eye_mask()
    diagonal = jnp.where(eye, matrix, 0.0)
    row = lax.rsqrt(jnp.sum(diagonal, axis=0, keepdims=True))
    column = lax.rsqrt(jnp.sum(diagonal, axis=1, keepdims=True))
    scaled = matrix * row * column
    bound = jnp.max(jnp.sum(jnp.abs(scaled), axis=0, keepdims=True), axis=1, keepdims=True)
    alpha = 1.0 / bound
    unit = jnp.where(eye, 1.0, 0.0)
    return scaled, row, column, alpha * unit, unit - alpha * scaled


def inverse_step(x, r):
    out = mm(jnp.concatenate([x, r], axis=0), r)
    return x + out[:R], out[R:]


def inverse_polish(scaled, x):
    residual = jnp.where(eye_mask(), 1.0, 0.0) - mm(scaled, x)
    return x + mm(x, residual)


def encode(x, dst):
    top = jnp.max(jnp.abs(x), axis=0, keepdims=True)
    code = jnp.ceil(jnp.log(jnp.maximum(top, 1e-30)) * 64.0)
    factor = jnp.exp(code * (-1.0 / 64.0)) * LEVELS
    dst[:PIECE] = jnp.round(x * factor).astype(jnp.int32).astype(jnp.int16)
    dst[PIECE:] = jnp.broadcast_to(code, (16, R)).astype(jnp.int32).astype(jnp.int16)


def decode(src):
    scale = decode_scale(src[PIECE:])
    return src[:PIECE].astype(F32) * scale


def decode_scale(code_rows):
    return jnp.exp(code_rows.astype(F32)[:1] * (1.0 / 64.0)) * (1.0 / LEVELS)


def main_kernel(
    x_hbm, v_ref, h_ref, w_ref, count_ref, trim_ref,
    nmt_ref, sums_ref,
    xv, dsend, drecv, keep, rs_send, rs_recv, acc, agbuf, st, gram, gs, qs, f_own, f_sib, ft, zb, us,
    wall, mix, cinv, wt, bpart, brecv, ball, e_gram, e_gram_sib, e_all, e_part, e_sib, e_half, e_recv, e_out, e_fin,
    xsem, d_s, d_r, rs_s, rs_r, ag_s, ag_r, fw_s, fw_r, w_s, w_r, b1_s, b1_r, b2_s, b2_r,
    e1_s, e1_r, e2_s, e2_r, e3_s, e3_r, f_s, f_r, eg_s, eg_r,
):
    run = lax.axis_index("run")
    me = lax.axis_index("mz")
    chip = lax.div(me, 2)
    core = lax.rem(me, 2)
    sibling = (run, chip * 2 + 1 - core)

    def chip_at(step):
        return lax.rem(chip + step, CHIPS)

    def peer(step):
        return (run, chip_at(step) * 2 + core)

    def run_peer(step):
        return (lax.rem(run + step, N_RUN), me)

    barrier = pltpu.get_barrier_semaphore()
    pl.semaphore_signal(barrier, inc=1, device_id=sibling, device_id_type=MESH)
    for step in FAR_FIRST:
        pl.semaphore_signal(barrier, inc=1, device_id=peer(step), device_id_type=MESH)
        pl.semaphore_signal(barrier, inc=1, device_id=run_peer(step), device_id_type=MESH)

    def x_chunk(step, side):
        return chip_at(step + 1) * 2 + (core if side else 1 - core)

    def x_copy(step, side):
        rows = pl.ds(pl.multiple_of(x_chunk(step, side) * OWN * BLOCK, BLOCK), OWN * BLOCK)
        return pltpu.make_async_copy(x_hbm.at[rows], xv.at[rows], xsem.at[step * 2 + side])

    for step in range(CHIPS):
        x_copy(step, 0).start()
        x_copy(step, 1).start()

    weights = jnp.concatenate([w_ref[...], jnp.zeros((16 - RUN_DEV, R), F32)], axis=0)
    wall[run] = weights

    def partial_body(step, carry):
        x_copy(step, 0).wait()
        x_copy(step, 1).wait()
        for i in range(OWN):
            t = i * CHIPS + step
            outs = []
            for side in range(2):
                first = pl.multiple_of((x_chunk(step, side) * OWN + i) * BLOCK, BLOCK)
                outs.append(
                    jnp.dot(xv[pl.ds(first, BLOCK), :], v_ref[...], preferred_element_type=F32)
                )
            encode(outs[0], dsend.at[t])
            keep[t] = outs[1]
        return carry

    lax.fori_loop(0, CHIPS, partial_body, 0)

    pl.semaphore_wait(barrier, 2 * CHIPS - 1)

    def send(src, dst, s_sem, r_sem, device):
        return pltpu.make_async_remote_copy(
            src_ref=src, dst_ref=dst, send_sem=s_sem, recv_sem=r_sem,
            device_id=device, device_id_type=MESH,
        )

    def run_from(step):
        return lax.rem(run + N_RUN - step, N_RUN)

    def chip_from(step):
        return lax.rem(chip + CHIPS - step, CHIPS)

    def w_copy(step, slot=run):
        return send(wall.at[slot], wall.at[slot], w_s.at[step], w_r.at[step], run_peer(step))

    def d_copy(t):
        return send(dsend.at[t], drecv.at[t], d_s.at[t], d_r.at[t], sibling)

    def rs_copy(t):
        return send(rs_send.at[t], rs_recv.at[t], rs_s.at[t], rs_r.at[t], peer(lax.rem(t, CHIPS) + 1))

    def d_start(b):
        for i in range(CHIPS):
            d_copy(b * CHIPS + i).start()

    def rs_encode(b):
        for i in range(CHIPS):
            d_copy(b * CHIPS + i).wait_recv()
        for i in range(CHIPS - 1):
            t = b * CHIPS + i
            encode(keep[t] + decode(drecv.at[t]), rs_send.at[t])
        t = b * CHIPS + CHIPS - 1
        acc[b] = keep[t] + decode(drecv.at[t])

    def rs_start(b):
        for i in range(CHIPS - 1):
            rs_copy(b * CHIPS + i).start()

    d_start(0)
    for step in range(1, N_RUN):
        w_copy(step).start()
    rs_encode(0)
    d_start(1)
    rs_start(0)
    d_start(2)
    rs_encode(1)

    for step in range(1, N_RUN):
        w_copy(step, run_from(step)).wait_recv()
    all_weights = wall[...].reshape(N_RUN * 16, R)
    h = h_ref[...]
    ht = h.T
    mix[...] = mm(ht, h)
    c_matrix = mm(all_weights.T, all_weights) * mix[...]
    scaled, row, column, x0, r0 = inverse_start(c_matrix)

    def inv_body(i, carry):
        return inverse_step(*carry)

    x0, r0 = lax.fori_loop(0, INV_STEPS[0], inv_body, (x0, r0))
    rs_start(1)
    rs_encode(2)
    x0, r0 = lax.fori_loop(0, INV_STEPS[1], inv_body, (x0, r0))
    rs_start(2)
    x0, r0 = lax.fori_loop(0, INV_STEPS[2], inv_body, (x0, r0))
    x0 = inverse_polish(scaled, x0)
    x0 = inverse_polish(scaled, x0)
    cinv[...] = x0 * row * column
    own_weights = jnp.concatenate([weights, jnp.zeros((R - 16, R), F32)], axis=0)
    wt[...] = own_weights.T

    starts = []
    total = jnp.int32(0)
    for k in range(RUN_DEV):
        starts.append(total)
        total = total + count_ref[0, k]
    ends = starts[1:] + [total]
    scans = lax.broadcasted_iota(jnp.int32, (BLOCK, R), 0)

    def shifted(offset, sign):
        dz, dx = offset
        z = lax.rem(lax.div(chip, 2) + 4 + sign * dz, 4)
        return z * 2 + lax.rem(lax.rem(chip, 2) + dx, 2)

    def ag_copy(i, b, slot=me):
        device = (run, shifted(OFFSETS[i], 1) * 2 + core)
        part = agbuf.at[slot, b]
        return send(part, part, ag_s.at[i * OWN + b], ag_r.at[i * OWN + b], device)

    def source(i):
        return chip if i == CHIPS - 1 else shifted(OFFSETS[i], -1)

    def fw_copy(i, b, side=core):
        part = agbuf.at[source(i) * 2 + side, b]
        return send(part, part, fw_s.at[i * OWN + b], fw_r.at[i * OWN + b], sibling)

    def unpack(slot, b):
        block = slot * OWN + b
        values = decode(agbuf.at[slot, b])
        hi0, lo0 = split(values[:R])
        hi1, lo1 = split(values[R:])
        both = jnp.concatenate(
            [jnp.concatenate([hi0, hi1], axis=1), jnp.concatenate([lo0, lo1], axis=1)], axis=0
        )
        st[block] = both
        return block, both

    def take_pair(i, b):
        fw_copy(i, b, 1 - core).wait_recv()
        pair = [unpack(source(i) * 2 + side, b) for side in (core, 1 - core)]
        for block, both in pair:
            out = lax.dot_general(both, both, (((1,), (1,)), ((), ())), preferred_element_type=F32)
            gram[block] = (out[:R, :R] + out[R:, R:]) + (out[:R, R:] + out[R:, :R])

    for b in range(OWN):
        own = acc[b]
        for i in range(CHIPS - 1):
            rs_copy(b * CHIPS + i).wait_recv()
        for i in range(CHIPS - 1):
            own = own + decode(rs_recv.at[b * CHIPS + i])
        block = me * OWN + b
        limit = jnp.int32(BLOCK)
        for k in range(RUN_DEV):
            limit = limit - jnp.where(block == ends[k] - 1, trim_ref[0, k], 0)
        own = jnp.where(scans < limit, own, 0.0)
        encode(jnp.concatenate([own[:R].T, own[R:].T], axis=0), agbuf.at[me, b])
        for i in range(CHIPS - 1):
            ag_copy(i, b).start()
        fw_copy(CHIPS - 1, b).start()
        if b:
            take_pair(CHIPS - 1, b - 1)

    take_pair(CHIPS - 1, OWN - 1)
    late = []
    for b in range(OWN):
        for i in range(CHIPS - 1):
            ag_copy(i, b, source(i) * 2 + core).wait_recv()
            fw_copy(i, b).start()
            if late:
                take_pair(*late.pop())
            late.append((i, b))
    take_pair(*late.pop())

    h = h_ref[...]
    eye = eye_mask()
    unit = jnp.where(eye, 1.0, 0.0)

    first_run = core * PAIR_RUNS
    pair_runs = range(PAIR_RUNS)
    lefts, sums = [], []
    for j in pair_runs:
        k = first_run + j
        count = count_ref[0, k]
        start = jnp.int32(0)
        for i in range(RUN_DEV - 1):
            start = start + jnp.where(i < k, count_ref[0, i], 0)
        s = gram[jnp.minimum(start, SLOTS - 1)]
        for i in range(1, MAXB):
            s = s + jnp.where(i < count, gram[jnp.minimum(start + i, SLOTS - 1)], 0.0)
        sums.append(s)
        lefts.append(h * w_ref[pl.ds(k, 1), :])
    halves = [mm(lefts[j], sums[j]) for j in pair_runs]
    grams = [mm_nt(halves[j], lefts[j]) for j in pair_runs]
    for j in pair_runs:
        g = grams[j]
        square = jnp.sum(jnp.sum(jnp.where(eye, g, 0.0), axis=0, keepdims=True), axis=1, keepdims=True)
        inv_norm = lax.rsqrt(square + 1e-6)
        gs[j] = g * (inv_norm * inv_norm)
        qs[j] = unit * inv_norm

    def newton_body(i, carry):
        rights = [right_of(1.5 * unit - 0.5 * gs[j]) for j in pair_runs]
        outs = [times(gs[j], rights[j]) for j in pair_runs]
        news = [times(outs[j], rights[j]) for j in pair_runs]
        products = [times(qs[j], rights[j]) for j in pair_runs]
        for j in pair_runs:
            gs[j] = news[j]
            qs[j] = products[j]
        return carry

    for i in range(NSTEPS - 1):
        newton_body(i, 0)

    lasts = [mm(qs[j], 1.5 * unit - 0.5 * gs[j]) for j in pair_runs]
    lasts = [mm(lasts[j], h * w_ref[pl.ds(first_run + j, 1), :]) for j in pair_runs]
    for j in pair_runs:
        hi, lo = split(lasts[j])
        f_own[j, :R] = hi
        f_own[j, R:] = lo

    f_copy = send(f_own, f_sib, f_s, f_r, sibling)
    f_copy.start()
    for j in pair_runs:
        ft[first_run + j] = f_own[j]
    f_copy.wait_recv()
    for j in pair_runs:
        ft[PAIR_RUNS - first_run + j] = f_sib[j]

    def project(group):
        polars = []
        for u in range(8):
            block = group * 8 + u
            owner = jnp.int32(0)
            end = jnp.int32(0)
            for k in range(RUN_DEV - 1):
                end = end + count_ref[0, k]
                owner = owner + jnp.where(block >= end, 1, 0)
            factor = ft[owner]
            out = jnp.dot(
                jnp.concatenate([factor, factor], axis=1), st[block], preferred_element_type=F32
            )
            polars.append((out[:R] + out[R:]).astype(BF16))
        for u in range(8):
            block = group * 8 + u
            rows = slice(block * BLOCK, (block + 1) * BLOCK)
            zb[block] = jnp.dot(polars[u], xv[rows, :], preferred_element_type=F32)

    for group in range(SLOTS // 8):
        project(group)

    left_h = stack_left(h.T)
    bpart[...] = jnp.zeros_like(bpart)
    wcols = wt[...]

    def combine_one(k, start):
        count = count_ref[0, k]
        z = zb[jnp.minimum(start, SLOTS - 1)]
        for i in range(1, MAXB):
            z = z + jnp.where(i < count, zb[jnp.minimum(start + i, SLOTS - 1)], 0.0)
        u = wide(left_h, z)
        us[k] = u
        col = jnp.sum(
            jnp.where(lax.broadcasted_iota(jnp.int32, (R, R), 1) == k, wcols, 0.0), axis=1, keepdims=True
        )
        bpart[...] += (u * col).reshape(N_RUN, R // N_RUN, WIDTH)
        return start + count

    start = jnp.int32(0)
    for k in range(RUN_DEV):
        start = combine_one(k, start)

    def b1_copy(step):
        return send(
            bpart.at[lax.rem(run + step, N_RUN)], brecv.at[step], b1_s.at[step], b1_r.at[step], run_peer(step)
        )

    def b2_copy(step, slot=run):
        return send(ball.at[slot], ball.at[slot], b2_s.at[step], b2_r.at[step], run_peer(step))

    for step in FAR_FIRST:
        b1_copy(step).start()
    own = bpart[run]
    for step in range(1, N_RUN):
        b1_copy(step).wait_recv()
        own = own + brecv[step]
    ball[run] = own
    for step in FAR_FIRST:
        b2_copy(step).start()
    for step in range(1, N_RUN):
        b2_copy(step, run_from(step)).wait_recv()

    nmt = wide(stack_left(cinv[...]), ball[...].reshape(R, WIDTH))
    nmt_ref[...] = nmt

    e_gram[...] = self_gram(nmt)
    e1g = send(e_gram, e_gram_sib, eg_s, eg_r, sibling)
    e1g.start()
    columns = jnp.zeros((R, R), F32)
    lanes = lax.broadcasted_iota(jnp.int32, (R, R), 1)
    for k in range(RUN_DEV):
        col = jnp.sum(us[k] * nmt, axis=1, keepdims=True)
        columns = jnp.where(lanes == k, col, columns)
    e_part[...] = columns.T[:16]

    HALF = (R + 16) // 2
    e1 = send(e_part, e_sib, e1_s, e1_r, sibling)
    e1.start()
    e1g.wait_recv()
    e1.wait_recv()
    e_all[:R] = e_gram[...] + e_gram_sib[...]
    e_all[R:] = e_part[...] + e_sib[...]
    mine = pl.ds(pl.multiple_of(core * HALF, 8), HALF)
    e_half[...] = e_all[mine]

    def e2_copy(step, slot=chip):
        return send(e_half, e_recv.at[slot], e2_s.at[step], e2_r.at[step], peer(step))

    for step in FAR_FIRST:
        e2_copy(step).start()
    e_recv[chip] = e_half[...]
    for step in range(1, CHIPS):
        e2_copy(step, chip_from(step)).wait_recv()
    e_out[...] = jnp.sum(e_recv[...], axis=0)
    e3 = send(e_out, e_fin, e3_s, e3_r, sibling)
    e3.start()
    sums_ref[mine] = e_out[...]
    e3.wait_recv()
    other = pl.ds(pl.multiple_of((1 - core) * HALF, 8), HALF)
    sums_ref[other] = e_fin[...]
    sums_ref[:R] = sums_ref[:R] * mix[...]

    for step in range(1, N_RUN):
        w_copy(step).wait_send()
        b1_copy(step).wait_send()
        b2_copy(step).wait_send()
    for i in range(CHIPS - 1):
        e2_copy(i + 1).wait_send()
        for b in range(OWN):
            rs_copy(b * CHIPS + i).wait_send()
            ag_copy(i, b).wait_send()
    for i in range(CHIPS):
        for b in range(OWN):
            d_copy(b * CHIPS + i).wait_send()
            fw_copy(i, b).wait_send()
    e1.wait_send()
    e1g.wait_send()
    e3.wait_send()
    f_copy.wait_send()


def last_kernel(nmt_ref, sums_ref, nm_ref, nw_ref):
    nm_ref[...] = nmt_ref[...].T
    scaled, row, column, x, r = inverse_start(sums_ref[:R])

    def more(carry):
        step, x, r = carry
        return (step < 10) & (jnp.max(jnp.abs(r)) > 1e-6)

    def body(carry):
        step, x, r = carry
        for _ in range(4):
            x, r = inverse_step(x, r)
        return step + 1, x, r

    _, x, r = lax.while_loop(more, body, (jnp.int32(0), x, r))
    x = inverse_polish(scaled, x)
    nw_ref[...] = mm(sums_ref[R:], x * row * column)[:RUN_DEV]


def per_device(spectra, mz_factor, mixing, run_weights, block_count, trim_scans):
    vmem = pl.BlockSpec(memory_space=pltpu.VMEM)
    smem = pl.BlockSpec(memory_space=pltpu.SMEM)
    dma8 = pltpu.SemaphoreType.DMA((8,))
    dma = pltpu.SemaphoreType.DMA
    half = (R + 16) // 2
    nmt, sums = pl.pallas_call(
        main_kernel,
        out_shape=(
            jax.ShapeDtypeStruct((R, WIDTH), F32),
            jax.ShapeDtypeStruct((R + 16, R), F32),
        ),
        in_specs=[pl.BlockSpec(memory_space=pl.ANY), vmem, vmem, vmem, smem, smem],
        out_specs=(vmem, vmem),
        scratch_shapes=[
            pltpu.VMEM((SLOTS * BLOCK, WIDTH), BF16),
            pltpu.VMEM((PIECES, CODED, R), jnp.int16),
            pltpu.VMEM((PIECES, CODED, R), jnp.int16),
            pltpu.VMEM((PIECES, BLOCK, R), F32),
            pltpu.VMEM((PIECES, CODED, R), jnp.int16),
            pltpu.VMEM((PIECES, CODED, R), jnp.int16),
            pltpu.VMEM((OWN, BLOCK, R), F32),
            pltpu.VMEM((2 * CHIPS, OWN, CODED, R), jnp.int16),
            pltpu.VMEM((SLOTS, 2 * R, BLOCK), BF16),
            pltpu.VMEM((SLOTS, R, R), F32),
            pltpu.VMEM((PAIR_RUNS, R, R), F32),
            pltpu.VMEM((PAIR_RUNS, R, R), F32),
            pltpu.VMEM((PAIR_RUNS, 2 * R, R), BF16),
            pltpu.VMEM((PAIR_RUNS, 2 * R, R), BF16),
            pltpu.VMEM((RUN_DEV, 2 * R, R), BF16),
            pltpu.VMEM((SLOTS, R, WIDTH), F32),
            pltpu.VMEM((RUN_DEV, R, WIDTH), F32),
            pltpu.VMEM((N_RUN, 16, R), F32),
            pltpu.VMEM((R, R), F32),
            pltpu.VMEM((R, R), F32),
            pltpu.VMEM((R, R), F32),
            pltpu.VMEM((N_RUN, R // N_RUN, WIDTH), F32),
            pltpu.VMEM((N_RUN, R // N_RUN, WIDTH), F32),
            pltpu.VMEM((N_RUN, R // N_RUN, WIDTH), F32),
            pltpu.VMEM((R, R), F32),
            pltpu.VMEM((R, R), F32),
            pltpu.VMEM((R + 16, R), F32),
            pltpu.VMEM((16, R), F32),
            pltpu.VMEM((16, R), F32),
            pltpu.VMEM((half, R), F32),
            pltpu.VMEM((CHIPS, half, R), F32),
            pltpu.VMEM((half, R), F32),
            pltpu.VMEM((half, R), F32),
            dma((2 * CHIPS,)),
            dma((PIECES,)), dma((PIECES,)), dma((PIECES,)), dma((PIECES,)),
            dma((PIECES,)), dma((PIECES,)), dma((PIECES,)), dma((PIECES,)),
            dma8, dma8, dma8, dma8, dma8, dma8,
            dma, dma, dma8, dma8, dma, dma, dma, dma, dma, dma,
        ],
        compiler_params=pltpu.CompilerParams(
            collective_id=0, has_side_effects=True, vmem_limit_bytes=58 * 2**20
        ),
    )(spectra, mz_factor, mixing, run_weights, block_count, trim_scans)
    return pl.pallas_call(
        last_kernel,
        out_shape=(
            jax.ShapeDtypeStruct((WIDTH, R), F32),
            jax.ShapeDtypeStruct((RUN_DEV, R), F32),
        ),
        in_specs=[vmem, vmem],
        out_specs=(vmem, vmem),
    )(nmt, sums)


def solution(mesh):
    placed = (P("run", "mz"), P("mz", None), P(), P("run", None), P("run", None), P("run", None))
    return jax.shard_map(
        per_device,
        mesh=mesh,
        in_specs=placed,
        out_specs=(P("mz", None), P("run", None)),
        check_vma=False,
    )
```

```python
import functools

import jax
import jax.numpy as jnp
from jax import lax
from jax.experimental import pallas as pl
from jax.experimental.pallas import tpu as pltpu
from jax.sharding import PartitionSpec as P

R = 128
BLOCK = 256
NSTEPS = 8
RUN_DEV = 12
SLOTS = 48
MAXB = 8
CHIPS = 8
N_RUN = 8
OWN = 3
PIECES = CHIPS * OWN
PIECE = BLOCK
CODED = PIECE + 16
WIDTH = 256
LEVELS = 32000.0
INV_STEPS = (4, 11, 11)

PAIR_RUNS = RUN_DEV // 2

OFFSETS = ((1, 0), (3, 0), (0, 1), (2, 0), (1, 1), (3, 1), (2, 1))

FAR_FIRST = (4, 5, 3, 6, 2, 7, 1)

MESH = pl.DeviceIdType.MESH
F32 = jnp.float32
BF16 = jnp.bfloat16


def split(x):
    hi = x.astype(BF16)
    return hi, (x - hi.astype(F32)).astype(BF16)


def right_of(y):
    yh, yl = split(y)
    right = jnp.concatenate([yh, yl], axis=1)
    return jnp.concatenate([right, right], axis=0)


def times(x, right):
    xh, xl = split(x)
    out = jnp.dot(jnp.concatenate([xh, xl], axis=1), right, preferred_element_type=F32)
    return out[:, :R] + out[:, R:]


def mm(x, y):
    return times(x, right_of(y))


def mm_nt(x, y):
    xh, xl = split(x)
    yh, yl = split(y)
    right = jnp.concatenate(
        [jnp.concatenate([yh, yh], axis=1), jnp.concatenate([yl, yl], axis=1)], axis=0
    )
    out = lax.dot_general(
        jnp.concatenate([xh, xl], axis=1),
        right,
        (((1,), (1,)), ((), ())),
        preferred_element_type=F32,
    )
    return out[:, :R] + out[:, R:]


def stack_left(x):
    xh, xl = split(x)
    return jnp.concatenate(
        [jnp.concatenate([xh, xh], axis=1), jnp.concatenate([xl, xl], axis=1)], axis=0
    )


def wide(left, y):
    yh, yl = split(y)
    out = jnp.dot(left, jnp.concatenate([yh, yl], axis=0), preferred_element_type=F32)
    return out[:R] + out[R:]


def self_gram(x):
    xh, xl = split(x)
    both = jnp.concatenate([xh, xl], axis=0)
    out = lax.dot_general(both, both, (((1,), (1,)), ((), ())), preferred_element_type=F32)
    return out[:R, :R] + out[:R, R:] + out[R:, :R] + out[R:, R:]


def eye_mask():
    return lax.broadcasted_iota(jnp.int32, (R, R), 0) == lax.broadcasted_iota(jnp.int32, (R, R), 1)


def inverse_start(matrix):
    eye = eye_mask()
    diagonal = jnp.where(eye, matrix, 0.0)
    row = lax.rsqrt(jnp.sum(diagonal, axis=0, keepdims=True))
    column = lax.rsqrt(jnp.sum(diagonal, axis=1, keepdims=True))
    scaled = matrix * row * column
    bound = jnp.max(jnp.sum(jnp.abs(scaled), axis=0, keepdims=True), axis=1, keepdims=True)
    alpha = 1.0 / bound
    unit = jnp.where(eye, 1.0, 0.0)
    return scaled, row, column, alpha * unit, unit - alpha * scaled


def inverse_step(x, r):
    out = mm(jnp.concatenate([x, r], axis=0), r)
    return x + out[:R], out[R:]


def inverse_polish(scaled, x):
    residual = jnp.where(eye_mask(), 1.0, 0.0) - mm(scaled, x)
    return x + mm(x, residual)


def encode(x, dst):
    top = jnp.max(jnp.abs(x), axis=0, keepdims=True)
    code = jnp.ceil(jnp.log(jnp.maximum(top, 1e-30)) * 64.0)
    factor = jnp.exp(code * (-1.0 / 64.0)) * LEVELS
    dst[:PIECE] = jnp.round(x * factor).astype(jnp.int32).astype(jnp.int16)
    dst[PIECE:] = jnp.broadcast_to(code, (16, R)).astype(jnp.int32).astype(jnp.int16)


def decode(src):
    scale = decode_scale(src[PIECE:])
    return src[:PIECE].astype(F32) * scale


def decode_scale(code_rows):
    return jnp.exp(code_rows.astype(F32)[:1] * (1.0 / 64.0)) * (1.0 / LEVELS)


def main_kernel(
    x_hbm, v_ref, h_ref, w_ref, count_ref, trim_ref,
    nmt_ref, sums_ref,
    xv, dsend, drecv, keep, rs_send, rs_recv, acc, agbuf, st, gram, gs, qs, f_own, f_sib, ft, zb, us,
    wall, mix, cinv, wt, bpart, brecv, ball, e_gram, e_gram_sib, e_all, e_part, e_sib, e_half, e_recv, e_out, e_fin,
    xsem, d_s, d_r, rs_s, rs_r, ag_s, ag_r, fw_s, fw_r, w_s, w_r, b1_s, b1_r, b2_s, b2_r,
    e1_s, e1_r, e2_s, e2_r, e3_s, e3_r, f_s, f_r, eg_s, eg_r,
):
    run = lax.axis_index("run")
    me = lax.axis_index("mz")
    chip = lax.div(me, 2)
    core = lax.rem(me, 2)
    sibling = (run, chip * 2 + 1 - core)

    def chip_at(step):
        return lax.rem(chip + step, CHIPS)

    def peer(step):
        return (run, chip_at(step) * 2 + core)

    def run_peer(step):
        return (lax.rem(run + step, N_RUN), me)

    barrier = pltpu.get_barrier_semaphore()
    pl.semaphore_signal(barrier, inc=1, device_id=sibling, device_id_type=MESH)
    for step in FAR_FIRST:
        pl.semaphore_signal(barrier, inc=1, device_id=peer(step), device_id_type=MESH)
        pl.semaphore_signal(barrier, inc=1, device_id=run_peer(step), device_id_type=MESH)

    def x_chunk(step, side):
        return chip_at(step + 1) * 2 + (core if side else 1 - core)

    def x_copy(step, side):
        rows = pl.ds(pl.multiple_of(x_chunk(step, side) * OWN * BLOCK, BLOCK), OWN * BLOCK)
        return pltpu.make_async_copy(x_hbm.at[rows], xv.at[rows], xsem.at[step * 2 + side])

    for step in range(CHIPS):
        x_copy(step, 0).start()
        x_copy(step, 1).start()

    weights = jnp.concatenate([w_ref[...], jnp.zeros((16 - RUN_DEV, R), F32)], axis=0)
    wall[run] = weights

    def partial_body(step, carry):
        x_copy(step, 0).wait()
        x_copy(step, 1).wait()
        for i in range(OWN):
            t = i * CHIPS + step
            outs = []
            for side in range(2):
                first = pl.multiple_of((x_chunk(step, side) * OWN + i) * BLOCK, BLOCK)
                outs.append(
                    jnp.dot(xv[pl.ds(first, BLOCK), :], v_ref[...], preferred_element_type=F32)
                )
            encode(outs[0], dsend.at[t])
            keep[t] = outs[1]
        return carry

    lax.fori_loop(0, CHIPS, partial_body, 0)

    pl.semaphore_wait(barrier, 2 * CHIPS - 1)

    def send(src, dst, s_sem, r_sem, device):
        return pltpu.make_async_remote_copy(
            src_ref=src, dst_ref=dst, send_sem=s_sem, recv_sem=r_sem,
            device_id=device, device_id_type=MESH,
        )

    def run_from(step):
        return lax.rem(run + N_RUN - step, N_RUN)

    def chip_from(step):
        return lax.rem(chip + CHIPS - step, CHIPS)

    def w_copy(step, slot=run):
        return send(wall.at[slot], wall.at[slot], w_s.at[step], w_r.at[step], run_peer(step))

    def d_copy(t):
        return send(dsend.at[t], drecv.at[t], d_s.at[t], d_r.at[t], sibling)

    def rs_copy(t):
        return send(rs_send.at[t], rs_recv.at[t], rs_s.at[t], rs_r.at[t], peer(lax.rem(t, CHIPS) + 1))

    def d_start(b):
        for i in range(CHIPS):
            d_copy(b * CHIPS + i).start()

    def rs_encode(b):
        for i in range(CHIPS):
            d_copy(b * CHIPS + i).wait_recv()
        for i in range(CHIPS - 1):
            t = b * CHIPS + i
            encode(keep[t] + decode(drecv.at[t]), rs_send.at[t])
        t = b * CHIPS + CHIPS - 1
        acc[b] = keep[t] + decode(drecv.at[t])

    def rs_start(b):
        for i in range(CHIPS - 1):
            rs_copy(b * CHIPS + i).start()

    d_start(0)
    for step in range(1, N_RUN):
        w_copy(step).start()
    for part in (range(3), range(3, CHIPS - 1)):
        for i in part:
            d_copy(i).wait_recv()
        for i in part:
            encode(keep[i] + decode(drecv.at[i]), rs_send.at[i])
        for i in part:
            rs_copy(i).start()
    d_copy(CHIPS - 1).wait_recv()
    acc[0] = keep[CHIPS - 1] + decode(drecv.at[CHIPS - 1])
    d_start(1)
    d_start(2)
    rs_encode(1)

    for step in range(1, N_RUN):
        w_copy(step, run_from(step)).wait_recv()
    all_weights = wall[...].reshape(N_RUN * 16, R)
    h = h_ref[...]
    ht = h.T
    mix[...] = mm(ht, h)
    c_matrix = mm(all_weights.T, all_weights) * mix[...]
    scaled, row, column, x0, r0 = inverse_start(c_matrix)

    def inv_body(i, carry):
        return inverse_step(*carry)

    x0, r0 = lax.fori_loop(0, INV_STEPS[0], inv_body, (x0, r0))
    rs_start(1)
    rs_encode(2)
    x0, r0 = lax.fori_loop(0, INV_STEPS[1], inv_body, (x0, r0))
    rs_start(2)
    x0, r0 = lax.fori_loop(0, INV_STEPS[2], inv_body, (x0, r0))
    x0 = inverse_polish(scaled, x0)
    x0 = inverse_polish(scaled, x0)
    cinv[...] = x0 * row * column
    own_weights = jnp.concatenate([weights, jnp.zeros((R - 16, R), F32)], axis=0)
    wt[...] = own_weights.T

    starts = []
    total = jnp.int32(0)
    for k in range(RUN_DEV):
        starts.append(total)
        total = total + count_ref[0, k]
    ends = starts[1:] + [total]
    scans = lax.broadcasted_iota(jnp.int32, (BLOCK, R), 0)

    def shifted(offset, sign):
        dz, dx = offset
        z = lax.rem(lax.div(chip, 2) + 4 + sign * dz, 4)
        return z * 2 + lax.rem(lax.rem(chip, 2) + dx, 2)

    def ag_copy(i, b, slot=me):
        device = (run, shifted(OFFSETS[i], 1) * 2 + core)
        part = agbuf.at[slot, b]
        return send(part, part, ag_s.at[i * OWN + b], ag_r.at[i * OWN + b], device)

    def source(i):
        return chip if i == CHIPS - 1 else shifted(OFFSETS[i], -1)

    def fw_copy(i, b, side=core):
        part = agbuf.at[source(i) * 2 + side, b]
        return send(part, part, fw_s.at[i * OWN + b], fw_r.at[i * OWN + b], sibling)

    def unpack(slot, b):
        block = slot * OWN + b
        values = decode(agbuf.at[slot, b])
        hi0, lo0 = split(values[:R])
        hi1, lo1 = split(values[R:])
        both = jnp.concatenate(
            [jnp.concatenate([hi0, hi1], axis=1), jnp.concatenate([lo0, lo1], axis=1)], axis=0
        )
        st[block] = both
        return block, both

    def take_pair(i, b):
        fw_copy(i, b, 1 - core).wait_recv()
        pair = [unpack(source(i) * 2 + side, b) for side in (core, 1 - core)]
        for block, both in pair:
            out = lax.dot_general(both, both, (((1,), (1,)), ((), ())), preferred_element_type=F32)
            gram[block] = (out[:R, :R] + out[R:, R:]) + (out[:R, R:] + out[R:, :R])

    for b in range(OWN):
        own = acc[b]
        for i in range(CHIPS - 1):
            rs_copy(b * CHIPS + i).wait_recv()
        for i in range(CHIPS - 1):
            own = own + decode(rs_recv.at[b * CHIPS + i])
        block = me * OWN + b
        limit = jnp.int32(BLOCK)
        for k in range(RUN_DEV):
            limit = limit - jnp.where(block == ends[k] - 1, trim_ref[0, k], 0)
        own = jnp.where(scans < limit, own, 0.0)
        encode(jnp.concatenate([own[:R].T, own[R:].T], axis=0), agbuf.at[me, b])
        for i in range(CHIPS - 1):
            ag_copy(i, b).start()
        fw_copy(CHIPS - 1, b).start()
        if b:
            take_pair(CHIPS - 1, b - 1)

    take_pair(CHIPS - 1, OWN - 1)
    late = []
    for b in range(OWN):
        for i in range(CHIPS - 1):
            ag_copy(i, b, source(i) * 2 + core).wait_recv()
            fw_copy(i, b).start()
            if late:
                take_pair(*late.pop())
            late.append((i, b))
    take_pair(*late.pop())

    h = h_ref[...]
    eye = eye_mask()
    unit = jnp.where(eye, 1.0, 0.0)

    first_run = core * PAIR_RUNS
    pair_runs = range(PAIR_RUNS)
    lefts, sums = [], []
    for j in pair_runs:
        k = first_run + j
        count = count_ref[0, k]
        start = jnp.int32(0)
        for i in range(RUN_DEV - 1):
            start = start + jnp.where(i < k, count_ref[0, i], 0)
        s = gram[jnp.minimum(start, SLOTS - 1)]
        for i in range(1, MAXB):
            s = s + jnp.where(i < count, gram[jnp.minimum(start + i, SLOTS - 1)], 0.0)
        sums.append(s)
        lefts.append(h * w_ref[pl.ds(k, 1), :])
    halves = [mm(lefts[j], sums[j]) for j in pair_runs]
    grams = [mm_nt(halves[j], lefts[j]) for j in pair_runs]
    for j in pair_runs:
        g = grams[j]
        square = jnp.sum(jnp.sum(jnp.where(eye, g, 0.0), axis=0, keepdims=True), axis=1, keepdims=True)
        inv_norm = lax.rsqrt(square + 1e-6)
        gs[j] = g * (inv_norm * inv_norm)
        qs[j] = unit * inv_norm

    def newton_body(i, carry):
        rights = [right_of(1.5 * unit - 0.5 * gs[j]) for j in pair_runs]
        outs = [times(gs[j], rights[j]) for j in pair_runs]
        news = [times(outs[j], rights[j]) for j in pair_runs]
        products = [times(qs[j], rights[j]) for j in pair_runs]
        for j in pair_runs:
            gs[j] = news[j]
            qs[j] = products[j]
        return carry

    for i in range(NSTEPS - 1):
        newton_body(i, 0)

    lasts = [mm(qs[j], 1.5 * unit - 0.5 * gs[j]) for j in pair_runs]
    lasts = [mm(lasts[j], h * w_ref[pl.ds(first_run + j, 1), :]) for j in pair_runs]
    for j in pair_runs:
        hi, lo = split(lasts[j])
        f_own[j, :R] = hi
        f_own[j, R:] = lo

    f_copy = send(f_own, f_sib, f_s, f_r, sibling)
    f_copy.start()
    for j in pair_runs:
        ft[first_run + j] = f_own[j]
    f_copy.wait_recv()
    for j in pair_runs:
        ft[PAIR_RUNS - first_run + j] = f_sib[j]

    def project(group):
        polars = []
        for u in range(8):
            block = group * 8 + u
            owner = jnp.int32(0)
            end = jnp.int32(0)
            for k in range(RUN_DEV - 1):
                end = end + count_ref[0, k]
                owner = owner + jnp.where(block >= end, 1, 0)
            factor = ft[owner]
            out = jnp.dot(
                jnp.concatenate([factor, factor], axis=1), st[block], preferred_element_type=F32
            )
            polars.append((out[:R] + out[R:]).astype(BF16))
        for u in range(8):
            block = group * 8 + u
            rows = slice(block * BLOCK, (block + 1) * BLOCK)
            zb[block] = jnp.dot(polars[u], xv[rows, :], preferred_element_type=F32)

    for group in range(SLOTS // 8):
        project(group)

    left_h = stack_left(h.T)
    bpart[...] = jnp.zeros_like(bpart)
    wcols = wt[...]

    def combine_one(k, start):
        count = count_ref[0, k]
        z = zb[jnp.minimum(start, SLOTS - 1)]
        for i in range(1, MAXB):
            z = z + jnp.where(i < count, zb[jnp.minimum(start + i, SLOTS - 1)], 0.0)
        u = wide(left_h, z)
        us[k] = u
        col = jnp.sum(
            jnp.where(lax.broadcasted_iota(jnp.int32, (R, R), 1) == k, wcols, 0.0), axis=1, keepdims=True
        )
        bpart[...] += (u * col).reshape(N_RUN, R // N_RUN, WIDTH)
        return start + count

    start = jnp.int32(0)
    for k in range(RUN_DEV):
        start = combine_one(k, start)

    def b1_copy(step):
        return send(
            bpart.at[lax.rem(run + step, N_RUN)], brecv.at[step], b1_s.at[step], b1_r.at[step], run_peer(step)
        )

    def b2_copy(step, slot=run):
        return send(ball.at[slot], ball.at[slot], b2_s.at[step], b2_r.at[step], run_peer(step))

    for step in FAR_FIRST:
        b1_copy(step).start()
    own = bpart[run]
    for step in range(1, N_RUN):
        b1_copy(step).wait_recv()
        own = own + brecv[step]
    ball[run] = own
    for step in FAR_FIRST:
        b2_copy(step).start()
    for step in range(1, N_RUN):
        b2_copy(step, run_from(step)).wait_recv()

    nmt = wide(stack_left(cinv[...]), ball[...].reshape(R, WIDTH))
    nmt_ref[...] = nmt

    e_gram[...] = self_gram(nmt)
    e1g = send(e_gram, e_gram_sib, eg_s, eg_r, sibling)
    e1g.start()
    columns = jnp.zeros((R, R), F32)
    lanes = lax.broadcasted_iota(jnp.int32, (R, R), 1)
    for k in range(RUN_DEV):
        col = jnp.sum(us[k] * nmt, axis=1, keepdims=True)
        columns = jnp.where(lanes == k, col, columns)
    e_part[...] = columns.T[:16]

    HALF = (R + 16) // 2
    e1 = send(e_part, e_sib, e1_s, e1_r, sibling)
    e1.start()
    e1g.wait_recv()
    e1.wait_recv()
    e_all[:R] = e_gram[...] + e_gram_sib[...]
    e_all[R:] = e_part[...] + e_sib[...]
    mine = pl.ds(pl.multiple_of(core * HALF, 8), HALF)
    e_half[...] = e_all[mine]

    def e2_copy(step, slot=chip):
        return send(e_half, e_recv.at[slot], e2_s.at[step], e2_r.at[step], peer(step))

    for step in FAR_FIRST:
        e2_copy(step).start()
    e_recv[chip] = e_half[...]
    for step in range(1, CHIPS):
        e2_copy(step, chip_from(step)).wait_recv()
    e_out[...] = jnp.sum(e_recv[...], axis=0)
    e3 = send(e_out, e_fin, e3_s, e3_r, sibling)
    e3.start()
    sums_ref[mine] = e_out[...]
    e3.wait_recv()
    other = pl.ds(pl.multiple_of((1 - core) * HALF, 8), HALF)
    sums_ref[other] = e_fin[...]
    sums_ref[:R] = sums_ref[:R] * mix[...]

    for step in range(1, N_RUN):
        w_copy(step).wait_send()
        b1_copy(step).wait_send()
        b2_copy(step).wait_send()
    for i in range(CHIPS - 1):
        e2_copy(i + 1).wait_send()
        for b in range(OWN):
            rs_copy(b * CHIPS + i).wait_send()
            ag_copy(i, b).wait_send()
    for i in range(CHIPS):
        for b in range(OWN):
            d_copy(b * CHIPS + i).wait_send()
            fw_copy(i, b).wait_send()
    e1.wait_send()
    e1g.wait_send()
    e3.wait_send()
    f_copy.wait_send()


def last_kernel(nmt_ref, sums_ref, nm_ref, nw_ref):
    nm_ref[...] = nmt_ref[...].T
    scaled, row, column, x, r = inverse_start(sums_ref[:R])

    def more(carry):
        step, x, r = carry
        return (step < 10) & (jnp.max(jnp.abs(r)) > 1e-6)

    def body(carry):
        step, x, r = carry
        for _ in range(4):
            x, r = inverse_step(x, r)
        return step + 1, x, r

    _, x, r = lax.while_loop(more, body, (jnp.int32(0), x, r))
    x = inverse_polish(scaled, x)
    nw_ref[...] = mm(sums_ref[R:], x * row * column)[:RUN_DEV]


def per_device(spectra, mz_factor, mixing, run_weights, block_count, trim_scans):
    vmem = pl.BlockSpec(memory_space=pltpu.VMEM)
    smem = pl.BlockSpec(memory_space=pltpu.SMEM)
    dma8 = pltpu.SemaphoreType.DMA((8,))
    dma = pltpu.SemaphoreType.DMA
    half = (R + 16) // 2
    nmt, sums = pl.pallas_call(
        main_kernel,
        out_shape=(
            jax.ShapeDtypeStruct((R, WIDTH), F32),
            jax.ShapeDtypeStruct((R + 16, R), F32),
        ),
        in_specs=[pl.BlockSpec(memory_space=pl.ANY), vmem, vmem, vmem, smem, smem],
        out_specs=(vmem, vmem),
        scratch_shapes=[
            pltpu.VMEM((SLOTS * BLOCK, WIDTH), BF16),
            pltpu.VMEM((PIECES, CODED, R), jnp.int16),
            pltpu.VMEM((PIECES, CODED, R), jnp.int16),
            pltpu.VMEM((PIECES, BLOCK, R), F32),
            pltpu.VMEM((PIECES, CODED, R), jnp.int16),
            pltpu.VMEM((PIECES, CODED, R), jnp.int16),
            pltpu.VMEM((OWN, BLOCK, R), F32),
            pltpu.VMEM((2 * CHIPS, OWN, CODED, R), jnp.int16),
            pltpu.VMEM((SLOTS, 2 * R, BLOCK), BF16),
            pltpu.VMEM((SLOTS, R, R), F32),
            pltpu.VMEM((PAIR_RUNS, R, R), F32),
            pltpu.VMEM((PAIR_RUNS, R, R), F32),
            pltpu.VMEM((PAIR_RUNS, 2 * R, R), BF16),
            pltpu.VMEM((PAIR_RUNS, 2 * R, R), BF16),
            pltpu.VMEM((RUN_DEV, 2 * R, R), BF16),
            pltpu.VMEM((SLOTS, R, WIDTH), F32),
            pltpu.VMEM((RUN_DEV, R, WIDTH), F32),
            pltpu.VMEM((N_RUN, 16, R), F32),
            pltpu.VMEM((R, R), F32),
            pltpu.VMEM((R, R), F32),
            pltpu.VMEM((R, R), F32),
            pltpu.VMEM((N_RUN, R // N_RUN, WIDTH), F32),
            pltpu.VMEM((N_RUN, R // N_RUN, WIDTH), F32),
            pltpu.VMEM((N_RUN, R // N_RUN, WIDTH), F32),
            pltpu.VMEM((R, R), F32),
            pltpu.VMEM((R, R), F32),
            pltpu.VMEM((R + 16, R), F32),
            pltpu.VMEM((16, R), F32),
            pltpu.VMEM((16, R), F32),
            pltpu.VMEM((half, R), F32),
            pltpu.VMEM((CHIPS, half, R), F32),
            pltpu.VMEM((half, R), F32),
            pltpu.VMEM((half, R), F32),
            dma((2 * CHIPS,)),
            dma((PIECES,)), dma((PIECES,)), dma((PIECES,)), dma((PIECES,)),
            dma((PIECES,)), dma((PIECES,)), dma((PIECES,)), dma((PIECES,)),
            dma8, dma8, dma8, dma8, dma8, dma8,
            dma, dma, dma8, dma8, dma, dma, dma, dma, dma, dma,
        ],
        compiler_params=pltpu.CompilerParams(
            collective_id=0, has_side_effects=True, vmem_limit_bytes=58 * 2**20
        ),
    )(spectra, mz_factor, mixing, run_weights, block_count, trim_scans)
    return pl.pallas_call(
        last_kernel,
        out_shape=(
            jax.ShapeDtypeStruct((WIDTH, R), F32),
            jax.ShapeDtypeStruct((RUN_DEV, R), F32),
        ),
        in_specs=[vmem, vmem],
        out_specs=(vmem, vmem),
    )(nmt, sums)


def solution(mesh):
    placed = (P("run", "mz"), P("mz", None), P(), P("run", None), P("run", None), P("run", None))
    return jax.shard_map(
        per_device,
        mesh=mesh,
        in_specs=placed,
        out_specs=(P("mz", None), P("run", None)),
        check_vma=False,
    )
```

```python
import functools

import jax
import jax.numpy as jnp
from jax import lax
from jax.experimental import pallas as pl
from jax.experimental.pallas import tpu as pltpu
from jax.sharding import PartitionSpec as P

R = 128
BLOCK = 256
NSTEPS = 8
RUN_DEV = 12
SLOTS = 48
MAXB = 8
CHIPS = 8
N_RUN = 8
OWN = 3
PIECES = CHIPS * OWN
PIECE = BLOCK
CODED = PIECE + 16
WIDTH = 256
LEVELS = 32000.0
INV_STEPS = (4, 11, 11)

PAIR_RUNS = RUN_DEV // 2

OFFSETS = ((1, 0), (3, 0), (0, 1), (2, 0), (1, 1), (3, 1), (2, 1))

FAR_FIRST = (4, 5, 3, 6, 2, 7, 1)

MESH = pl.DeviceIdType.MESH
F32 = jnp.float32
BF16 = jnp.bfloat16


def split(x):
    hi = x.astype(BF16)
    return hi, (x - hi.astype(F32)).astype(BF16)


def right_of(y):
    yh, yl = split(y)
    right = jnp.concatenate([yh, yl], axis=1)
    return jnp.concatenate([right, right], axis=0)


def times(x, right):
    xh, xl = split(x)
    out = jnp.dot(jnp.concatenate([xh, xl], axis=1), right, preferred_element_type=F32)
    return out[:, :R] + out[:, R:]


def mm(x, y):
    return times(x, right_of(y))


def mm_nt(x, y):
    xh, xl = split(x)
    yh, yl = split(y)
    right = jnp.concatenate(
        [jnp.concatenate([yh, yh], axis=1), jnp.concatenate([yl, yl], axis=1)], axis=0
    )
    out = lax.dot_general(
        jnp.concatenate([xh, xl], axis=1),
        right,
        (((1,), (1,)), ((), ())),
        preferred_element_type=F32,
    )
    return out[:, :R] + out[:, R:]


def stack_left(x):
    xh, xl = split(x)
    return jnp.concatenate(
        [jnp.concatenate([xh, xh], axis=1), jnp.concatenate([xl, xl], axis=1)], axis=0
    )


def wide(left, y):
    yh, yl = split(y)
    out = jnp.dot(left, jnp.concatenate([yh, yl], axis=0), preferred_element_type=F32)
    return out[:R] + out[R:]


def self_gram(x):
    xh, xl = split(x)
    both = jnp.concatenate([xh, xl], axis=0)
    out = lax.dot_general(both, both, (((1,), (1,)), ((), ())), preferred_element_type=F32)
    return out[:R, :R] + out[:R, R:] + out[R:, :R] + out[R:, R:]


def eye_mask():
    return lax.broadcasted_iota(jnp.int32, (R, R), 0) == lax.broadcasted_iota(jnp.int32, (R, R), 1)


def inverse_start(matrix):
    eye = eye_mask()
    diagonal = jnp.where(eye, matrix, 0.0)
    row = lax.rsqrt(jnp.sum(diagonal, axis=0, keepdims=True))
    column = lax.rsqrt(jnp.sum(diagonal, axis=1, keepdims=True))
    scaled = matrix * row * column
    bound = jnp.max(jnp.sum(jnp.abs(scaled), axis=0, keepdims=True), axis=1, keepdims=True)
    alpha = 1.0 / bound
    unit = jnp.where(eye, 1.0, 0.0)
    return scaled, row, column, alpha * unit, unit - alpha * scaled


def inverse_step(x, r):
    out = mm(jnp.concatenate([x, r], axis=0), r)
    return x + out[:R], out[R:]


def inverse_polish(scaled, x):
    residual = jnp.where(eye_mask(), 1.0, 0.0) - mm(scaled, x)
    return x + mm(x, residual)


def encode(x, dst):
    top = jnp.max(jnp.abs(x), axis=0, keepdims=True)
    code = jnp.ceil(jnp.log(jnp.maximum(top, 1e-30)) * 64.0)
    factor = jnp.exp(code * (-1.0 / 64.0)) * LEVELS
    dst[:PIECE] = jnp.round(x * factor).astype(jnp.int32).astype(jnp.int16)
    dst[PIECE:] = jnp.broadcast_to(code, (16, R)).astype(jnp.int32).astype(jnp.int16)


def decode(src):
    scale = decode_scale(src[PIECE:])
    return src[:PIECE].astype(F32) * scale


def decode_scale(code_rows):
    return jnp.exp(code_rows.astype(F32)[:1] * (1.0 / 64.0)) * (1.0 / LEVELS)


def main_kernel(
    x_hbm, v_ref, h_ref, w_ref, count_ref, trim_ref,
    nmt_ref, sums_ref,
    xv, dsend, drecv, keep, rs_send, rs_recv, acc, agbuf, st, gram, gs, qs, f_own, f_sib, ft, zb, us,
    wall, mix, cinv, wt, bpart, brecv, ball, e_gram, e_gram_sib, e_all, e_part, e_sib, e_half, e_recv, e_out, e_fin,
    xsem, d_s, d_r, rs_s, rs_r, ag_s, ag_r, fw_s, fw_r, w_s, w_r, b1_s, b1_r, b2_s, b2_r,
    e1_s, e1_r, e2_s, e2_r, e3_s, e3_r, f_s, f_r, eg_s, eg_r,
):
    run = lax.axis_index("run")
    me = lax.axis_index("mz")
    chip = lax.div(me, 2)
    core = lax.rem(me, 2)
    sibling = (run, chip * 2 + 1 - core)

    def chip_at(step):
        return lax.rem(chip + step, CHIPS)

    def peer(step):
        return (run, chip_at(step) * 2 + core)

    def run_peer(step):
        return (lax.rem(run + step, N_RUN), me)

    barrier = pltpu.get_barrier_semaphore()
    pl.semaphore_signal(barrier, inc=1, device_id=sibling, device_id_type=MESH)
    for step in FAR_FIRST:
        pl.semaphore_signal(barrier, inc=1, device_id=peer(step), device_id_type=MESH)
        pl.semaphore_signal(barrier, inc=1, device_id=run_peer(step), device_id_type=MESH)

    def x_chunk(step, side):
        return chip_at(step + 1) * 2 + (core if side else 1 - core)

    def x_copy(step, side):
        rows = pl.ds(pl.multiple_of(x_chunk(step, side) * OWN * BLOCK, BLOCK), OWN * BLOCK)
        return pltpu.make_async_copy(x_hbm.at[rows], xv.at[rows], xsem.at[step * 2 + side])

    for step in range(CHIPS):
        x_copy(step, 0).start()
        x_copy(step, 1).start()

    weights = jnp.concatenate([w_ref[...], jnp.zeros((16 - RUN_DEV, R), F32)], axis=0)
    wall[run] = weights

    def partial_body(step, carry):
        x_copy(step, 0).wait()
        x_copy(step, 1).wait()
        for i in range(OWN):
            t = i * CHIPS + step
            outs = []
            for side in range(2):
                first = pl.multiple_of((x_chunk(step, side) * OWN + i) * BLOCK, BLOCK)
                outs.append(
                    jnp.dot(xv[pl.ds(first, BLOCK), :], v_ref[...], preferred_element_type=F32)
                )
            encode(outs[0], dsend.at[t])
            keep[t] = outs[1]
        return carry

    lax.fori_loop(0, CHIPS, partial_body, 0)

    pl.semaphore_wait(barrier, 2 * CHIPS - 1)

    def send(src, dst, s_sem, r_sem, device):
        return pltpu.make_async_remote_copy(
            src_ref=src, dst_ref=dst, send_sem=s_sem, recv_sem=r_sem,
            device_id=device, device_id_type=MESH,
        )

    def run_from(step):
        return lax.rem(run + N_RUN - step, N_RUN)

    def chip_from(step):
        return lax.rem(chip + CHIPS - step, CHIPS)

    def w_copy(step, slot=run):
        return send(wall.at[slot], wall.at[slot], w_s.at[step], w_r.at[step], run_peer(step))

    def d_copy(t):
        return send(dsend.at[t], drecv.at[t], d_s.at[t], d_r.at[t], sibling)

    def rs_copy(t):
        return send(rs_send.at[t], rs_recv.at[t], rs_s.at[t], rs_r.at[t], peer(lax.rem(t, CHIPS) + 1))

    def d_start(b):
        for i in range(CHIPS):
            d_copy(b * CHIPS + i).start()

    def rs_encode(b):
        for i in range(CHIPS):
            d_copy(b * CHIPS + i).wait_recv()
        for i in range(CHIPS - 1):
            t = b * CHIPS + i
            encode(keep[t] + decode(drecv.at[t]), rs_send.at[t])
        t = b * CHIPS + CHIPS - 1
        acc[b] = keep[t] + decode(drecv.at[t])

    def rs_start(b):
        for i in range(CHIPS - 1):
            rs_copy(b * CHIPS + i).start()

    d_start(0)
    for step in range(1, N_RUN):
        w_copy(step).start()
    for part in (range(3), range(3, CHIPS - 1)):
        for i in part:
            d_copy(i).wait_recv()
        for i in part:
            encode(keep[i] + decode(drecv.at[i]), rs_send.at[i])
        for i in part:
            rs_copy(i).start()
    d_copy(CHIPS - 1).wait_recv()
    acc[0] = keep[CHIPS - 1] + decode(drecv.at[CHIPS - 1])
    d_start(1)
    d_start(2)
    rs_encode(1)

    for step in range(1, N_RUN):
        w_copy(step, run_from(step)).wait_recv()
    all_weights = wall[...].reshape(N_RUN * 16, R)
    h = h_ref[...]
    ht = h.T
    mix[...] = mm(ht, h)
    c_matrix = mm(all_weights.T, all_weights) * mix[...]
    scaled, row, column, x0, r0 = inverse_start(c_matrix)

    def inv_body(i, carry):
        return inverse_step(*carry)

    x0, r0 = lax.fori_loop(0, INV_STEPS[0], inv_body, (x0, r0))
    rs_start(1)
    rs_encode(2)
    x0, r0 = lax.fori_loop(0, INV_STEPS[1], inv_body, (x0, r0))
    rs_start(2)
    x0, r0 = lax.fori_loop(0, INV_STEPS[2], inv_body, (x0, r0))
    x0 = inverse_polish(scaled, x0)
    x0 = inverse_polish(scaled, x0)
    cinv[...] = x0 * row * column
    own_weights = jnp.concatenate([weights, jnp.zeros((R - 16, R), F32)], axis=0)
    wt[...] = own_weights.T

    starts = []
    total = jnp.int32(0)
    for k in range(RUN_DEV):
        starts.append(total)
        total = total + count_ref[0, k]
    ends = starts[1:] + [total]
    scans = lax.broadcasted_iota(jnp.int32, (BLOCK, R), 0)

    def shifted(offset, sign):
        dz, dx = offset
        z = lax.rem(lax.div(chip, 2) + 4 + sign * dz, 4)
        return z * 2 + lax.rem(lax.rem(chip, 2) + dx, 2)

    def ag_copy(i, b, slot=me):
        device = (run, shifted(OFFSETS[i], 1) * 2 + core)
        part = agbuf.at[slot, b]
        return send(part, part, ag_s.at[i * OWN + b], ag_r.at[i * OWN + b], device)

    def source(i):
        return chip if i == CHIPS - 1 else shifted(OFFSETS[i], -1)

    def fw_copy(i, b, side=core):
        part = agbuf.at[source(i) * 2 + side, b]
        return send(part, part, fw_s.at[i * OWN + b], fw_r.at[i * OWN + b], sibling)

    def unpack(slot, b):
        block = slot * OWN + b
        values = decode(agbuf.at[slot, b])
        hi0, lo0 = split(values[:R])
        hi1, lo1 = split(values[R:])
        both = jnp.concatenate(
            [jnp.concatenate([hi0, hi1], axis=1), jnp.concatenate([lo0, lo1], axis=1)], axis=0
        )
        st[block] = both
        return block, both

    def take_pair(i, b):
        fw_copy(i, b, 1 - core).wait_recv()
        pair = [unpack(source(i) * 2 + side, b) for side in (core, 1 - core)]
        for block, both in pair:
            out = lax.dot_general(both, both, (((1,), (1,)), ((), ())), preferred_element_type=F32)
            gram[block] = (out[:R, :R] + out[R:, R:]) + (out[:R, R:] + out[R:, :R])

    for b in range(OWN):
        own = acc[b]
        for i in range(CHIPS - 1):
            rs_copy(b * CHIPS + i).wait_recv()
        for i in range(CHIPS - 1):
            own = own + decode(rs_recv.at[b * CHIPS + i])
        block = me * OWN + b
        limit = jnp.int32(BLOCK)
        for k in range(RUN_DEV):
            limit = limit - jnp.where(block == ends[k] - 1, trim_ref[0, k], 0)
        own = jnp.where(scans < limit, own, 0.0)
        encode(jnp.concatenate([own[:R].T, own[R:].T], axis=0), agbuf.at[me, b])
        for i in range(CHIPS - 1):
            ag_copy(i, b).start()
        fw_copy(CHIPS - 1, b).start()
        if b:
            take_pair(CHIPS - 1, b - 1)

    take_pair(CHIPS - 1, OWN - 1)
    late = []
    for b in range(OWN):
        for i in range(CHIPS - 1):
            ag_copy(i, b, source(i) * 2 + core).wait_recv()
            fw_copy(i, b).start()
            if late:
                take_pair(*late.pop())
            late.append((i, b))
    take_pair(*late.pop())

    h = h_ref[...]
    eye = eye_mask()
    unit = jnp.where(eye, 1.0, 0.0)

    first_run = core * PAIR_RUNS
    pair_runs = range(PAIR_RUNS)
    lefts, sums = [], []
    for j in pair_runs:
        k = first_run + j
        count = count_ref[0, k]
        start = jnp.int32(0)
        for i in range(RUN_DEV - 1):
            start = start + jnp.where(i < k, count_ref[0, i], 0)
        s = gram[jnp.minimum(start, SLOTS - 1)]
        for i in range(1, MAXB):
            s = s + jnp.where(i < count, gram[jnp.minimum(start + i, SLOTS - 1)], 0.0)
        sums.append(s)
        lefts.append(h * w_ref[pl.ds(k, 1), :])
    halves = [mm(lefts[j], sums[j]) for j in pair_runs]
    grams = [mm_nt(halves[j], lefts[j]) for j in pair_runs]
    for j in pair_runs:
        g = grams[j]
        square = jnp.sum(jnp.sum(jnp.where(eye, g, 0.0), axis=0, keepdims=True), axis=1, keepdims=True)
        inv_norm = lax.rsqrt(square + 1e-6)
        gs[j] = g * (inv_norm * inv_norm)
        qs[j] = unit * inv_norm

    def newton_body(i, carry):
        rights = [right_of(1.5 * unit - 0.5 * gs[j]) for j in pair_runs]
        outs = [times(gs[j], rights[j]) for j in pair_runs]
        news = [times(outs[j], rights[j]) for j in pair_runs]
        products = [times(qs[j], rights[j]) for j in pair_runs]
        for j in pair_runs:
            gs[j] = news[j]
            qs[j] = products[j]
        return carry

    for i in range(NSTEPS - 1):
        newton_body(i, 0)

    lasts = [mm(qs[j], 1.5 * unit - 0.5 * gs[j]) for j in pair_runs]
    lasts = [mm(lasts[j], h * w_ref[pl.ds(first_run + j, 1), :]) for j in pair_runs]
    for j in pair_runs:
        hi, lo = split(lasts[j])
        f_own[j, :R] = hi
        f_own[j, R:] = lo

    f_copy = send(f_own, f_sib, f_s, f_r, sibling)
    f_copy.start()
    for j in pair_runs:
        ft[first_run + j] = f_own[j]
    f_copy.wait_recv()
    for j in pair_runs:
        ft[PAIR_RUNS - first_run + j] = f_sib[j]

    def project(group):
        polars = []
        for u in range(12):
            block = group * 12 + u
            owner = jnp.int32(0)
            end = jnp.int32(0)
            for k in range(RUN_DEV - 1):
                end = end + count_ref[0, k]
                owner = owner + jnp.where(block >= end, 1, 0)
            factor = ft[owner]
            out = jnp.dot(
                jnp.concatenate([factor, factor], axis=1), st[block], preferred_element_type=F32
            )
            polars.append((out[:R] + out[R:]).astype(BF16))
        for u in range(12):
            block = group * 12 + u
            rows = slice(block * BLOCK, (block + 1) * BLOCK)
            zb[block] = jnp.dot(polars[u], xv[rows, :], preferred_element_type=F32)

    for group in range(SLOTS // 12):
        project(group)

    left_h = stack_left(h.T)
    bpart[...] = jnp.zeros_like(bpart)
    wcols = wt[...]

    def combine_one(k, start):
        count = count_ref[0, k]
        z = zb[jnp.minimum(start, SLOTS - 1)]
        for i in range(1, MAXB):
            z = z + jnp.where(i < count, zb[jnp.minimum(start + i, SLOTS - 1)], 0.0)
        u = wide(left_h, z)
        us[k] = u
        col = jnp.sum(
            jnp.where(lax.broadcasted_iota(jnp.int32, (R, R), 1) == k, wcols, 0.0), axis=1, keepdims=True
        )
        bpart[...] += (u * col).reshape(N_RUN, R // N_RUN, WIDTH)
        return start + count

    start = jnp.int32(0)
    for k in range(RUN_DEV):
        start = combine_one(k, start)

    def b1_copy(step):
        return send(
            bpart.at[lax.rem(run + step, N_RUN)], brecv.at[step], b1_s.at[step], b1_r.at[step], run_peer(step)
        )

    def b2_copy(step, slot=run):
        return send(ball.at[slot], ball.at[slot], b2_s.at[step], b2_r.at[step], run_peer(step))

    for step in FAR_FIRST:
        b1_copy(step).start()
    own = bpart[run]
    for step in range(1, N_RUN):
        b1_copy(step).wait_recv()
        own = own + brecv[step]
    ball[run] = own
    for step in FAR_FIRST:
        b2_copy(step).start()
    for step in range(1, N_RUN):
        b2_copy(step, run_from(step)).wait_recv()

    nmt = wide(stack_left(cinv[...]), ball[...].reshape(R, WIDTH))
    nmt_ref[...] = nmt

    e_gram[...] = self_gram(nmt)
    e1g = send(e_gram, e_gram_sib, eg_s, eg_r, sibling)
    e1g.start()
    columns = jnp.zeros((R, R), F32)
    lanes = lax.broadcasted_iota(jnp.int32, (R, R), 1)
    for k in range(RUN_DEV):
        col = jnp.sum(us[k] * nmt, axis=1, keepdims=True)
        columns = jnp.where(lanes == k, col, columns)
    e_part[...] = columns.T[:16]

    HALF = (R + 16) // 2
    e1 = send(e_part, e_sib, e1_s, e1_r, sibling)
    e1.start()
    e1g.wait_recv()
    e1.wait_recv()
    e_all[:R] = e_gram[...] + e_gram_sib[...]
    e_all[R:] = e_part[...] + e_sib[...]
    mine = pl.ds(pl.multiple_of(core * HALF, 8), HALF)
    e_half[...] = e_all[mine]

    def e2_copy(step, slot=chip):
        return send(e_half, e_recv.at[slot], e2_s.at[step], e2_r.at[step], peer(step))

    for step in FAR_FIRST:
        e2_copy(step).start()
    e_recv[chip] = e_half[...]
    for step in range(1, CHIPS):
        e2_copy(step, chip_from(step)).wait_recv()
    e_out[...] = jnp.sum(e_recv[...], axis=0)
    e3 = send(e_out, e_fin, e3_s, e3_r, sibling)
    e3.start()
    sums_ref[mine] = e_out[...]
    e3.wait_recv()
    other = pl.ds(pl.multiple_of((1 - core) * HALF, 8), HALF)
    sums_ref[other] = e_fin[...]
    sums_ref[:R] = sums_ref[:R] * mix[...]

    for step in range(1, N_RUN):
        w_copy(step).wait_send()
        b1_copy(step).wait_send()
        b2_copy(step).wait_send()
    for i in range(CHIPS - 1):
        e2_copy(i + 1).wait_send()
        for b in range(OWN):
            rs_copy(b * CHIPS + i).wait_send()
            ag_copy(i, b).wait_send()
    for i in range(CHIPS):
        for b in range(OWN):
            d_copy(b * CHIPS + i).wait_send()
            fw_copy(i, b).wait_send()
    e1.wait_send()
    e1g.wait_send()
    e3.wait_send()
    f_copy.wait_send()


def last_kernel(nmt_ref, sums_ref, nm_ref, nw_ref):
    nm_ref[...] = nmt_ref[...].T
    scaled, row, column, x, r = inverse_start(sums_ref[:R])

    def more(carry):
        step, x, r = carry
        return (step < 10) & (jnp.max(jnp.abs(r)) > 1e-6)

    def body(carry):
        step, x, r = carry
        for _ in range(4):
            x, r = inverse_step(x, r)
        return step + 1, x, r

    _, x, r = lax.while_loop(more, body, (jnp.int32(0), x, r))
    x = inverse_polish(scaled, x)
    nw_ref[...] = mm(sums_ref[R:], x * row * column)[:RUN_DEV]


def per_device(spectra, mz_factor, mixing, run_weights, block_count, trim_scans):
    vmem = pl.BlockSpec(memory_space=pltpu.VMEM)
    smem = pl.BlockSpec(memory_space=pltpu.SMEM)
    dma8 = pltpu.SemaphoreType.DMA((8,))
    dma = pltpu.SemaphoreType.DMA
    half = (R + 16) // 2
    nmt, sums = pl.pallas_call(
        main_kernel,
        out_shape=(
            jax.ShapeDtypeStruct((R, WIDTH), F32),
            jax.ShapeDtypeStruct((R + 16, R), F32),
        ),
        in_specs=[pl.BlockSpec(memory_space=pl.ANY), vmem, vmem, vmem, smem, smem],
        out_specs=(vmem, vmem),
        scratch_shapes=[
            pltpu.VMEM((SLOTS * BLOCK, WIDTH), BF16),
            pltpu.VMEM((PIECES, CODED, R), jnp.int16),
            pltpu.VMEM((PIECES, CODED, R), jnp.int16),
            pltpu.VMEM((PIECES, BLOCK, R), F32),
            pltpu.VMEM((PIECES, CODED, R), jnp.int16),
            pltpu.VMEM((PIECES, CODED, R), jnp.int16),
            pltpu.VMEM((OWN, BLOCK, R), F32),
            pltpu.VMEM((2 * CHIPS, OWN, CODED, R), jnp.int16),
            pltpu.VMEM((SLOTS, 2 * R, BLOCK), BF16),
            pltpu.VMEM((SLOTS, R, R), F32),
            pltpu.VMEM((PAIR_RUNS, R, R), F32),
            pltpu.VMEM((PAIR_RUNS, R, R), F32),
            pltpu.VMEM((PAIR_RUNS, 2 * R, R), BF16),
            pltpu.VMEM((PAIR_RUNS, 2 * R, R), BF16),
            pltpu.VMEM((RUN_DEV, 2 * R, R), BF16),
            pltpu.VMEM((SLOTS, R, WIDTH), F32),
            pltpu.VMEM((RUN_DEV, R, WIDTH), F32),
            pltpu.VMEM((N_RUN, 16, R), F32),
            pltpu.VMEM((R, R), F32),
            pltpu.VMEM((R, R), F32),
            pltpu.VMEM((R, R), F32),
            pltpu.VMEM((N_RUN, R // N_RUN, WIDTH), F32),
            pltpu.VMEM((N_RUN, R // N_RUN, WIDTH), F32),
            pltpu.VMEM((N_RUN, R // N_RUN, WIDTH), F32),
            pltpu.VMEM((R, R), F32),
            pltpu.VMEM((R, R), F32),
            pltpu.VMEM((R + 16, R), F32),
            pltpu.VMEM((16, R), F32),
            pltpu.VMEM((16, R), F32),
            pltpu.VMEM((half, R), F32),
            pltpu.VMEM((CHIPS, half, R), F32),
            pltpu.VMEM((half, R), F32),
            pltpu.VMEM((half, R), F32),
            dma((2 * CHIPS,)),
            dma((PIECES,)), dma((PIECES,)), dma((PIECES,)), dma((PIECES,)),
            dma((PIECES,)), dma((PIECES,)), dma((PIECES,)), dma((PIECES,)),
            dma8, dma8, dma8, dma8, dma8, dma8,
            dma, dma, dma8, dma8, dma, dma, dma, dma, dma, dma,
        ],
        compiler_params=pltpu.CompilerParams(
            collective_id=0, has_side_effects=True, vmem_limit_bytes=58 * 2**20
        ),
    )(spectra, mz_factor, mixing, run_weights, block_count, trim_scans)
    return pl.pallas_call(
        last_kernel,
        out_shape=(
            jax.ShapeDtypeStruct((WIDTH, R), F32),
            jax.ShapeDtypeStruct((RUN_DEV, R), F32),
        ),
        in_specs=[vmem, vmem],
        out_specs=(vmem, vmem),
    )(nmt, sums)


def solution(mesh):
    placed = (P("run", "mz"), P("mz", None), P(), P("run", None), P("run", None), P("run", None))
    return jax.shard_map(
        per_device,
        mesh=mesh,
        in_specs=placed,
        out_specs=(P("mz", None), P("run", None)),
        check_vma=False,
    )
```
